32 devices in a mesh: groups: 2 (over x), ctx: 2 (over core), tp: 8 (over z, y).
Axes of the slice: x: 2, y: 2, z: 4, core: 2. Of those that a mesh axis runs over, the one named last changes fastest.
Arguments:
- hidden_in: bfloat16 [2048, 8192], P(('groups', 'ctx'), 'tp'), parts along dimension 0, may hold values from -20 to 20
- attn_gain: bfloat16 [8192], replicated, may hold values from 0.5 to 1.5
- query_weight: bfloat16 [8192, 4096], P(None, 'tp'), may hold values from -0.0625 to 0.0625
- keys: bfloat16 [16384, 512], P(('groups', 'ctx')), parts along dimension 0, may hold values from -300 to 300
- values: bfloat16 [16384, 512], P(('groups', 'ctx')), parts along dimension 0, may hold values from -6 to 6
- offset: int32 [2], P('groups'), parts along dimension 0, may hold values from 4096 to 7168
- out_weight: bfloat16 [4096, 8192], P('tp'), may hold values from -1 to 1
- sign_bits: int32 [8192], replicated, may hold values from 0 to 1
- attn_exps: int32 [64, 64], P(('groups', 'ctx')), parts along dimension 0, may hold values from -8 to -5
- norm_gain: bfloat16 [8192], replicated, may hold values from 0.25 to 1.75
- norm_exps: int32 [64, 64], P(('groups', 'ctx')), parts along dimension 0, may hold values from -6 to -4
Outputs:
- normed: bfloat16 [2048, 8192], P(('groups', 'ctx')), parts along dimension 0
The draws below stay inside these ranges and needn't reach their ends.
There are 2 independent parts, one for each index of `groups`. The reference program is written for one: setup_inputs(seed, part) draws one part's arguments, and reference() takes and returns one part's arrays. A program takes and returns all parts, laid end to end along the dimension named above; an argument that names none is the same for every part. Nothing has to cross between parts.
Inputs may be any that keep to these rules, and one draw needn't show every extreme that they name: `offset`: every query row sees all of the first 4096 context positions.
All inputs are finite; a program needn't handle non-finite values.
Results may differ from the reference program's by a relative error of at most 0.014.
The reference program's roundings to bfloat16 on the way count: a program that leaves them out, or rounds other values in their place, can miss the bound.
Values may be sent and summed in bfloat16 or wider, within the bound.
No kernel may reach another device: no remote copies, remote signals or barrier semaphores. Data moves between devices by JAX's collectives and lax.ppermute only.
A program may use at most 256 MiB of HBM per device.

```python
import math
import jax
import jax.numpy as jnp
from jax import lax

D = 8192
HD = 128
HEADS = 32
KVH = 4
HB = 128
RB = 32
S_DEV = 4096
Q_TOK = 1024
CTX = 8192
N_CTX = 2
N_TP = 8


def draw_hidden_in(key, part):
    key = jax.random.fold_in(key, 11)
    first_key, second_key, third_key = jax.random.split(key, 3)
    columns = jnp.arange(D, dtype=jnp.float32) / D
    col_scale = 10.0 ** (0.5 * columns + 0.5 * jax.random.uniform(second_key, (D,), dtype=jnp.float32))
    row_scale = 10.0 ** (0.5 * jax.random.uniform(third_key, (Q_TOK, 1), dtype=jnp.float32))
    base = jax.random.truncated_normal(first_key, -4.0, 4.0, (Q_TOK, D), dtype=jnp.float32)
    return (0.15 * base * col_scale * row_scale).astype(jnp.bfloat16)


def draw_keys(key, part):
    key = jax.random.fold_in(key, 23)
    first_key = jax.random.fold_in(key, 0)
    result = 2.0 * jax.random.truncated_normal(first_key, -4.0, 4.0, (CTX, KVH * HD), dtype=jnp.float32)
    return result.astype(jnp.bfloat16)


def plant(array, key, least, high):
    extent = array.shape
    index_at = [jax.random.randint(jax.random.fold_in(key, axis), (), 0, extent[axis]) for axis in range(len(extent))]
    array = array.at[tuple(index_at)].set(least)
    longest = extent.index(max(extent))
    index_at[longest] = (index_at[longest] + 1) % extent[longest]
    return array.at[tuple(index_at)].set(high)


def strengthened(entries, rng, source, target, parts, factor):
    def block_of(dim):
        return (jnp.arange(entries.shape[dim]) // (entries.shape[dim] // parts)).reshape((-1,) + (1,) * (entries.ndim - 1 - dim))

    near = jax.random.permutation(rng, parts)[block_of(target)]
    other_side = (block_of(target) + parts // 2) % parts
    return jnp.where((block_of(source) == near) | (block_of(source) == other_side), factor * entries, entries)


def shard_levels(stream_key, shape, cuts, low, largest):
    def one(dim, blocks):
        steps = jax.random.uniform(jax.random.fold_in(jax.random.fold_in(stream_key, 6), dim), (blocks,), jnp.float32, low / len(cuts), largest / len(cuts))
        return jnp.repeat(jnp.exp(steps), shape[dim] // blocks).reshape((-1,) + (1,) * (len(shape) - dim - 1))

    level = one(*cuts[0])
    for cut in cuts[1:]:
        level = level * one(*cut)
    return level


def normal_values(own_key, dims, width, reach, cuts=(), kind=jnp.bfloat16):
    level = shard_levels(own_key, dims, cuts, -0.22, 0.18) if cuts else 1.0
    drawn = jax.random.normal(own_key, dims, jnp.float32) * width * level
    return jnp.minimum(jnp.maximum(drawn, -reach), reach).astype(kind)


def heavy_noise(key, shape, spread, bound, cuts, heavy, held_as=jnp.bfloat16):
    values = spread * jax.random.normal(key, shape, jnp.float32)
    if cuts:
        values = values * shard_levels(key, shape, cuts, -0.22, 0.18)
    return jnp.clip(strengthened(values, jax.random.fold_in(key, 3), *heavy), -bound, bound).astype(held_as)


def setup_inputs(seed: int = 0, part: int = 0) -> dict:
    key_of = jax.random.split(jax.random.key(seed), 12)
    part_splits = jax.random.split(jax.random.fold_in(key_of[11], part), 12)
    hidden_in = draw_hidden_in(jax.random.fold_in(jax.random.fold_in(key_of[11], part), 71), part)
    attn_gain = jnp.clip(1.0 + 0.1 * jax.random.normal(key_of[1], (D,), jnp.float32), 0.5, 1.5).astype(jnp.bfloat16)
    query_weight = normal_values(key_of[2], (D, HEADS * HD), D ** -0.5, 0.0625, ((1, 8),))
    keys = draw_keys(jax.random.fold_in(jax.random.fold_in(key_of[11], part), 71), part)
    values = normal_values(part_splits[4], (CTX, KVH * HD), 1.0, 6.0, ((0, 2),))
    offset = jax.random.randint(part_splits[5], (1,), S_DEV, CTX - Q_TOK + 1).astype(jnp.int32)
    out_weight = heavy_noise(key_of[6], (HEADS * HD, D), (HD // 2) ** -0.5, 1.0, ((0, 8),), (0, 1, 8, 2.0))
    sign_bits = plant(jax.random.randint(key_of[7], (D,), 0, 2), jax.random.fold_in(key_of[7], 1), 0, 1).astype(jnp.int32)
    attn_exps = plant(jax.random.randint(part_splits[8], (Q_TOK // RB, D // HB), -8, -4), jax.random.fold_in(part_splits[8], 1), -8, (-4) - 1).astype(jnp.int32)
    norm_gain = jnp.clip(1.0 + 0.15 * jax.random.normal(key_of[9], (D,), jnp.float32), 0.25, 1.75).astype(jnp.bfloat16)
    norm_exps = plant(jax.random.randint(part_splits[10], (Q_TOK // RB, D // HB), -6, -3), jax.random.fold_in(part_splits[10], 1), -6, (-3) - 1).astype(jnp.int32)
    return dict(hidden_in=hidden_in, attn_gain=attn_gain, query_weight=query_weight, keys=keys, values=values, offset=offset, out_weight=out_weight, sign_bits=sign_bits, attn_exps=attn_exps, norm_gain=norm_gain, norm_exps=norm_exps)


def hadamard_table(order):
    table = jnp.ones((1, 1), dtype=jnp.float32)
    while table.shape[0] < order:
        upper = jnp.concatenate([table, table], axis=1)
        lower = jnp.concatenate([table, -table], axis=1)
        table = jnp.concatenate([upper, lower], axis=0)
    return table

def rotary(vectors, positions):
    half_dim = vectors.shape[-1] // 2
    inv_freq = jnp.exp(-(jnp.arange(half_dim, dtype=jnp.float32) * (2.0 / vectors.shape[-1])) * math.log(500000.0))
    angles = positions.astype(jnp.float32)[:, None] * inv_freq[None, :]
    cosine = jnp.cos(angles)
    sine_vals = jnp.sin(angles)
    first_half = vectors[..., :half_dim]
    second_half = vectors[..., half_dim:]
    return jnp.concatenate([first_half * cosine - second_half * sine_vals, second_half * cosine + first_half * sine_vals], axis=-1)

def encode(partial_value, sign_vector, exps, hadamard):
    row_count = partial_value.shape[0]
    blocks = (partial_value * sign_vector).reshape(row_count, -1, hadamard.shape[0])
    spun = jnp.einsum('rbi,ij->rbj', blocks, hadamard, precision=lax.Precision.HIGHEST) * (1.0 / math.sqrt(hadamard.shape[0]))
    coded = jnp.clip(spun * jnp.exp2(-exps.astype(jnp.float32))[..., None], -127.0, 127.0)
    return coded.reshape(row_count, -1)

def decode(summed, sign_vector, exps, hadamard):
    row_count = summed.shape[0]
    blocks = summed.reshape(row_count, -1, hadamard.shape[0]) * jnp.exp2(exps.astype(jnp.float32))[..., None]
    spun = jnp.einsum('rbi,ij->rbj', blocks, hadamard, precision=lax.Precision.HIGHEST) * (1.0 / math.sqrt(hadamard.shape[0]))
    return spun.reshape(row_count, -1) * sign_vector

def reference(hidden_in, attn_gain, query_weight, keys, values, offset, out_weight, sign_bits, attn_exps, norm_gain, norm_exps):
    features = hidden_in.astype(jnp.float32)
    mean_in = lax.optimization_barrier(jnp.sum(features * features, axis=1, keepdims=True)) / D
    normed_in = (features * lax.rsqrt(mean_in + 1e-05) * attn_gain.astype(jnp.float32)).astype(jnp.bfloat16)
    projected_q = jnp.dot(normed_in, query_weight, preferred_element_type=jnp.float32)
    query_pos = offset[0].astype(jnp.int32) + jnp.arange(Q_TOK, dtype=jnp.int32)
    heads_q = projected_q.reshape(Q_TOK, HEADS, HD).transpose(1, 0, 2)
    rotated = rotary(heads_q, query_pos).astype(jnp.bfloat16)
    key_pos = jnp.arange(CTX, dtype=jnp.int32)
    visible = key_pos[None, :] <= query_pos[:, None]
    mask_blocks = visible.reshape(Q_TOK, N_CTX, S_DEV)
    group_size = HEADS // KVH

    def one_head(item):
        query_head, head_index = item
        column = (head_index // group_size * HD).astype(jnp.int32)
        key_head = lax.dynamic_slice_in_dim(keys, column, HD, 1)
        value_head = lax.dynamic_slice_in_dim(values, column, HD, 1)
        scores = jnp.dot(query_head, key_head.T, preferred_element_type=jnp.float32) * (1.0 / math.sqrt(HD))
        scores = jnp.where(visible, scores, -1e+30).reshape(Q_TOK, N_CTX, S_DEV)
        maxima = lax.optimization_barrier(jnp.max(scores, axis=2))
        weights_f = jnp.where(mask_blocks, jnp.exp(scores - maxima[..., None]), 0.0)
        totals = lax.optimization_barrier(jnp.sum(weights_f, axis=2))
        weights_b = weights_f.astype(jnp.bfloat16)
        accumulated = jnp.einsum('qbs,bsd->qbd', weights_b.astype(jnp.float32), value_head.reshape(N_CTX, S_DEV, HD).astype(jnp.float32))
        overall = lax.optimization_barrier(jnp.max(maxima, axis=1))
        factors = jnp.exp(maxima - overall[:, None])
        mixed = lax.optimization_barrier(jnp.sum(factors[..., None] * accumulated, axis=1)) / lax.optimization_barrier(jnp.sum(factors * totals, axis=1))[:, None]
        return mixed.astype(jnp.bfloat16)
    attended = lax.map(one_head, (rotated, jnp.arange(HEADS, dtype=jnp.int32)))
    attended = attended.transpose(1, 0, 2).reshape(Q_TOK, HEADS * HD)
    hadamard = hadamard_table(HB)
    sign_vector = (2 * sign_bits - 1).astype(jnp.float32)
    e_rows = jnp.repeat(attn_exps, RB, axis=0)
    slab = HEADS // N_TP * HD

    def add_term(step, code_sum):
        start = step.astype(jnp.int32) * slab
        part_a = lax.dynamic_slice_in_dim(attended, start, slab, 1)
        part_w = lax.dynamic_slice_in_dim(out_weight, start, slab, 0)
        partial_value = jnp.dot(part_a, part_w, preferred_element_type=jnp.float32)
        coded = encode(partial_value, sign_vector, e_rows, hadamard).astype(jnp.bfloat16)
        coded = lax.optimization_barrier(coded)
        return code_sum + coded.astype(jnp.float32)
    code_sum = lax.fori_loop(0, N_TP, add_term, jnp.zeros((Q_TOK, D), jnp.float32))
    projected = decode(code_sum, sign_vector, e_rows, hadamard)
    residual = (features + projected).astype(jnp.bfloat16)
    resid_f = residual.astype(jnp.float32)
    mean_sq = lax.optimization_barrier(jnp.sum(resid_f * resid_f, axis=1, keepdims=True)) / D
    scaled = resid_f * lax.rsqrt(mean_sq + 1e-05) * norm_gain.astype(jnp.float32)
    norm_rows = jnp.repeat(norm_exps, RB, axis=0)
    norm_code = jnp.clip(scaled.reshape(Q_TOK, -1, HB) * jnp.exp2(-norm_rows.astype(jnp.float32))[..., None], -127.0, 127.0).astype(jnp.bfloat16)
    norm_code = lax.optimization_barrier(norm_code)
    decoded = norm_code.astype(jnp.float32) * jnp.exp2(norm_rows.astype(jnp.float32))[..., None]
    return decoded.reshape(Q_TOK, D).astype(jnp.bfloat16)
```

```python
import functools
import math

import jax
import jax.numpy as jnp
from jax import lax
from jax.experimental import pallas as pl
from jax.experimental.pallas import tpu as pltpu
from jax.sharding import PartitionSpec as P

HD = 128
KVH = 4
HB = 128
RB = 32
MIB = 1 << 20
EPS = 1e-05
LOG2E = math.log2(math.e)


def _params(mib, **kw):
    return pltpu.CompilerParams(vmem_limit_bytes=mib * MIB, **kw)


def _permute(value, axis, pairs):
    return lax.ppermute(value, axis, pairs)


def _both(value, axis, count):
    if count == 2:
        other = _permute(value, axis, [(0, 1), (1, 0)])
        first = lax.axis_index(axis) == 0
        return jnp.stack([jnp.where(first, value, other), jnp.where(first, other, value)])
    return lax.all_gather(value, axis, axis=0)


def _gather_line(value, zc, yc):
    n = zc * yc
    z = lax.axis_index("tp") // yc
    y = lax.axis_index("tp") % yc
    bar = lax.optimization_barrier

    def across(v):
        return _permute(v, "tp", [(s, s ^ 1) for s in range(n)])

    def up(v, k):
        return _permute(v, "tp", [(s, s + yc) for s in range(n) if k - 1 <= s // yc < zc - 1])

    def down(v, k):
        return _permute(v, "tp", [(s, s - yc) for s in range(n) if 1 <= s // yc <= zc - k])

    def stream(x):
        y0, u1, d1 = bar((across(x), up(x, 1), down(x, 1)))
        va = jnp.where(z == 0, d1, u1)
        ya, u2, d2 = bar((across(va), up(u1, 2), down(d1, 2)))
        vb = jnp.where(z == 0, d2, jnp.where(z == 3, u2, d1))
        yb, u3, d3 = bar((across(vb), up(u2, 3), down(d2, 3)))
        vc = jnp.where(z == 0, d3, jnp.where(z == 1, d2, jnp.where(z == 2, u2, u3)))
        return [x, va, vb, vc, y0, ya, yb, across(vc)]

    def pick(a, b, c, d):
        return jnp.where(z == 0, a, jnp.where(z == 1, b, jnp.where(z == 2, c, d)))

    layers = [z, pick(1, 0, 1, 2), pick(2, 2, 3, 1), pick(3, 3, 0, 0)]
    ids = [l * yc + y for l in layers] + [l * yc + (1 - y) for l in layers]
    half = value.shape[1] // 2
    left = stream(value[:, :half])
    right = stream(value[:, half:])
    return left, right, jnp.stack(ids).astype(jnp.int32)


def gather_tp(value, zc, yc):
    if zc == 4 and yc == 2:
        return _gather_line(value, zc, yc)
    n = zc * yc
    whole = lax.all_gather(value, "tp", axis=0)
    half = value.shape[1] // 2
    left = [whole[i, :, :half] for i in range(n)]
    right = [whole[i, :, half:] for i in range(n)]
    return left, right, jnp.arange(n, dtype=jnp.int32)


def _query_kernel(n, heads, ids, *refs):
    parts = refs[: 2 * n]
    gain, weight, cos, sin, out = refs[2 * n :]
    half = parts[0].shape[1]
    d = 2 * n * half
    total = None
    for p in parts:
        f = p[...].astype(jnp.float32)
        s = jnp.sum(f * f, axis=1, keepdims=True)
        total = s if total is None else total + s
    r = lax.rsqrt(total / d + EPS)
    acc = None
    for i in range(2 * n):
        side, slot = i // n, i % n
        at = ids[slot]
        f = parts[i][...].astype(jnp.float32)
        normed = (f * r * gain[2 * at + side]).astype(jnp.bfloat16)
        rows = pl.ds(pl.multiple_of(at * (2 * half) + side * half, half), half)
        t = jnp.dot(normed, weight[rows, :], preferred_element_type=jnp.float32)
        acc = t if acc is None else acc + t
    for h in range(heads):
        v = acc[:, h * HD : (h + 1) * HD]
        turned = v * cos[...] + pltpu.roll(v, HD // 2, 1) * sin[...]
        out[h] = turned.astype(jnp.bfloat16)


def project_queries(left, right, ids, gain, weight, cos, sin):
    n = len(left)
    rows, half = left[0].shape
    d, width = weight.shape
    heads = width // HD
    tile = 128
    gains = gain.astype(jnp.float32).reshape(2 * n, 1, half)
    grid_spec = pltpu.PrefetchScalarGridSpec(
        num_scalar_prefetch=1,
        grid=(rows // tile,),
        in_specs=[pl.BlockSpec((tile, half), lambda i, ids: (i, 0))] * (2 * n)
        + [
            pl.BlockSpec((2 * n, 1, half), lambda i, ids: (0, 0, 0)),
            pl.BlockSpec((d, width), lambda i, ids: (0, 0), pipeline_mode=pl.Buffered(1)),
            pl.BlockSpec((tile, HD), lambda i, ids: (i, 0)),
            pl.BlockSpec((tile, HD), lambda i, ids: (i, 0)),
        ],
        out_specs=pl.BlockSpec((heads, tile, HD), lambda i, ids: (0, i, 0)),
    )
    return pl.pallas_call(
        functools.partial(_query_kernel, n, heads),
        grid_spec=grid_spec,
        out_shape=jax.ShapeDtypeStruct((heads, rows, HD), jnp.bfloat16),
        compiler_params=_params(48),
        cost_estimate=pl.CostEstimate(
            flops=2 * rows * d * width, bytes_accessed=2 * (rows * d + d * width), transcendentals=0
        ),
        name="query_projection",
    )(ids, *left, *right, gains, weight, cos, sin)


CK = 512


def _attend_kernel(heads, tile, span, info, q_ref, k_ref, v_ref, out, s_ref, m_ref, l_ref, acc_ref):
    step = pl.program_id(0)
    scale = LOG2E / math.sqrt(HD)
    m = heads * tile
    q = q_ref[...].reshape(m, HD)
    first_pos = info[0] + step * tile
    row_pos = first_pos + lax.rem(lax.broadcasted_iota(jnp.int32, (m, CK), 0), tile)

    def scores(base, j, masked):
        keys = k_ref[pl.ds(pl.multiple_of(base + j * CK, CK), CK), :]
        s = lax.dot_general(q, keys, (((1,), (1,)), ((), ())), preferred_element_type=jnp.float32)
        if masked:
            col = base + j * CK + lax.broadcasted_iota(jnp.int32, (m, CK), 1)
            s = jnp.where(col <= row_pos, s, -1e30)
        s_ref[:, pl.ds(pl.multiple_of(j * CK, CK), CK)] = s
        top = m_ref[...]
        for c in range(CK // 128):
            top = jnp.maximum(top, s[:, c * 128 : (c + 1) * 128])
        m_ref[...] = top

    def weigh(base, j, top):
        s = s_ref[:, pl.ds(pl.multiple_of(j * CK, CK), CK)]
        p = jnp.exp2((s - top) * scale)
        total = l_ref[...]
        for c in range(CK // 128):
            total = total + p[:, c * 128 : (c + 1) * 128]
        l_ref[...] = total
        vals = v_ref[pl.ds(pl.multiple_of(base + j * CK, CK), CK), :]
        acc_ref[...] += jnp.dot(p.astype(jnp.bfloat16), vals, preferred_element_type=jnp.float32)

    def block(base, full, count):
        m_ref[...] = jnp.full(m_ref.shape, -1e30, jnp.float32)
        l_ref[...] = jnp.zeros(l_ref.shape, jnp.float32)
        acc_ref[...] = jnp.zeros(acc_ref.shape, jnp.float32)

        def loop(n, f):
            if isinstance(n, int):
                for j in range(n):
                    f(j)
            else:
                lax.fori_loop(0, n, lambda j, c: (f(j), c)[1], 0)

        loop(full, lambda j: scores(base, j, False))
        if count is not full:
            lax.fori_loop(full, count, lambda j, c: (scores(base, j, True), c)[1], 0)
        top = jnp.max(m_ref[...], axis=1, keepdims=True)
        loop(count, lambda j: weigh(base, j, top))
        return top, jnp.sum(l_ref[...], axis=1, keepdims=True), acc_ref[...]

    chunks = span // CK
    blocks = k_ref.shape[0] // span
    top, total, acc = block(0, chunks, chunks)
    for b in range(1, blocks):
        base = b * span
        full = jnp.clip((first_pos + 1 - base) // CK, 0, chunks)
        count = jnp.clip((first_pos + tile - 1 - base) // CK + 1, 0, chunks)
        top2, total2, acc2 = block(base, full, count)
        new = jnp.maximum(top, top2)
        f1 = jnp.exp2((top - new) * scale)
        f2 = jnp.exp2((top2 - new) * scale)
        acc = f1 * acc + f2 * acc2
        total = f1 * total + f2 * total2
        top = new
    res = (acc / total).astype(jnp.bfloat16)
    for h in range(heads):
        out[:, h * HD : (h + 1) * HD] = res[h * tile : (h + 1) * tile]


def attend(q, keys, values, start, span):
    heads, rows, _ = q.shape
    tile = min(512 // heads, rows)
    m = heads * tile
    total = keys.shape[0]
    grid_spec = pltpu.PrefetchScalarGridSpec(
        num_scalar_prefetch=1,
        grid=(rows // tile,),
        in_specs=[
            pl.BlockSpec((heads, tile, HD), lambda i, info: (0, i, 0)),
            pl.BlockSpec((total, HD), lambda i, info: (0, 0), pipeline_mode=pl.Buffered(1)),
            pl.BlockSpec((total, HD), lambda i, info: (0, 0), pipeline_mode=pl.Buffered(1)),
        ],
        out_specs=pl.BlockSpec((tile, heads * HD), lambda i, info: (i, 0)),
        scratch_shapes=[
            pltpu.VMEM((m, span), jnp.float32),
            pltpu.VMEM((m, 128), jnp.float32),
            pltpu.VMEM((m, 128), jnp.float32),
            pltpu.VMEM((m, HD), jnp.float32),
        ],
    )
    return pl.pallas_call(
        functools.partial(_attend_kernel, heads, tile, span),
        grid_spec=grid_spec,
        out_shape=jax.ShapeDtypeStruct((rows, heads * HD), jnp.bfloat16),
        compiler_params=_params(48),
        cost_estimate=pl.CostEstimate(
            flops=4 * heads * rows * total * HD, bytes_accessed=4 * total * HD, transcendentals=heads * rows * total
        ),
        name="attend",
    )(start, q, keys, values)


def _spin(x, table):
    hi = x.astype(jnp.bfloat16)
    lo = (x - hi.astype(jnp.float32)).astype(jnp.bfloat16)
    return jnp.dot(hi, table, preferred_element_type=jnp.float32) + jnp.dot(
        lo, table, preferred_element_type=jnp.float32
    )


def _by_row_block(x, scale):
    blocks = scale.shape[0]
    rows, cols = x.shape
    return (x.reshape(blocks, rows // blocks, cols) * scale[:, None, :]).reshape(rows, cols)


def _code_kernel(zc, info, *refs):
    atts = refs[:zc]
    own, far, table, sign, scale, out = refs[zc:]
    spin = table[...] * sign[...]
    csz, gsz = far.shape[0], far.shape[1]
    total = None
    for k in range(zc):
        if k == 0:
            w = own[...]
        else:
            w = jnp.concatenate([far[c, g, k - 1] for g in range(gsz) for c in range(csz)], axis=0)
        part = jnp.dot(atts[k][...], w, preferred_element_type=jnp.float32)
        spun = _spin(part, spin)
        coded = jnp.clip(_by_row_block(spun, scale[...]), -127.0, 127.0)
        coded = coded.astype(jnp.bfloat16).astype(jnp.float32)
        total = coded if total is None else total + coded
    out[...] = total.astype(out.dtype)


def code_terms(atts, own, far, table, signs, scale, z, side, out_type):
    zc = len(atts)
    rows, depth = atts[0].shape
    csz, gsz, _, piece, cols = far.shape
    width = cols // 2
    tile = table.shape[0]
    steps = width // tile
    info = jnp.stack([z * (cols // tile) + side * steps, side * steps]).astype(jnp.int32)
    grid_spec = pltpu.PrefetchScalarGridSpec(
        num_scalar_prefetch=1,
        grid=(steps,),
        in_specs=[pl.BlockSpec((rows, depth), lambda j, info: (0, 0), pipeline_mode=pl.Buffered(1))] * zc
        + [
            pl.BlockSpec((depth, tile), lambda j, info: (0, info[0] + j)),
            pl.BlockSpec((csz, gsz, zc - 1, piece, tile), lambda j, info: (0, 0, 0, 0, info[1] + j)),
            pl.BlockSpec((tile, tile), lambda j, info: (0, 0)),
            pl.BlockSpec((tile, 1), lambda j, info: (j, 0)),
            pl.BlockSpec((scale.shape[0], tile), lambda j, info: (0, j)),
        ],
        out_specs=pl.BlockSpec((rows, tile), lambda j, info: (0, j)),
    )
    return pl.pallas_call(
        functools.partial(_code_kernel, zc),
        grid_spec=grid_spec,
        out_shape=jax.ShapeDtypeStruct((rows, width), out_type),
        compiler_params=_params(48),
        cost_estimate=pl.CostEstimate(
            flops=2 * zc * rows * width * (depth + 2 * tile), bytes_accessed=2 * zc * depth * width, transcendentals=0
        ),
        name="code_terms",
    )(info, *atts, own, far, table, signs, scale)


def _residual_kernel(mine, theirs, hidden, table, scale, sign, out):
    summed = mine[...] + theirs[...].astype(jnp.float32)
    tile = table.shape[0]
    for j in range(summed.shape[1] // tile):
        at = slice(j * tile, (j + 1) * tile)
        spun = _spin(summed[:, at], table[...])
        projected = _by_row_block(spun, scale[:, at]) * sign[:, at]
        out[:, at] = (hidden[:, at].astype(jnp.float32) + projected).astype(jnp.bfloat16)


def add_residual(mine, theirs, hidden, table, scale, sign):
    rows, width = mine.shape
    tile = min(256, rows)
    blocks = scale.shape[0] * tile // rows
    return pl.pallas_call(
        _residual_kernel,
        grid=(rows // tile,),
        in_specs=[
            pl.BlockSpec((tile, width), lambda i: (i, 0)),
            pl.BlockSpec((tile, width), lambda i: (i, 0)),
            pl.BlockSpec((tile, width), lambda i: (i, 0)),
            pl.BlockSpec(table.shape, lambda i: (0, 0)),
            pl.BlockSpec((blocks, width), lambda i: (i, 0)),
            pl.BlockSpec((1, width), lambda i: (0, 0)),
        ],
        out_specs=pl.BlockSpec((tile, width), lambda i: (i, 0)),
        out_shape=jax.ShapeDtypeStruct((rows, width), jnp.bfloat16),
        compiler_params=_params(40),
        cost_estimate=pl.CostEstimate(
            flops=4 * rows * width * table.shape[0], bytes_accessed=10 * rows * width, transcendentals=0
        ),
        name="residual",
    )(mine, theirs, hidden, table, scale, sign)


def _norm_kernel(n, ids, *refs):
    parts = refs[: 2 * n]
    gain, down, up, out = refs[2 * n :]
    rows, half = parts[0].shape
    d = 2 * n * half
    total = None
    for p in parts:
        f = p[...].astype(jnp.float32)
        s = jnp.sum(f * f, axis=1, keepdims=True)
        total = s if total is None else total + s
    r = lax.rsqrt(total / d + EPS)
    for i in range(2 * n):
        side, slot = i // n, i % n
        at = 2 * ids[slot] + side
        scaled = parts[i][...].astype(jnp.float32) * r * gain[at]
        code = jnp.clip(_by_row_block(scaled, down[0, at]), -127.0, 127.0).astype(jnp.bfloat16)
        value = _by_row_block(code.astype(jnp.float32), up[0, at]).astype(jnp.bfloat16)
        out[:, pl.ds(pl.multiple_of(at * half, half), half)] = value


def norm_rows(left, right, ids, gain, exps):
    n = len(left)
    rows, half = left[0].shape
    d = 2 * n * half
    tile = 128
    steps = rows // tile
    blocks = tile // RB
    gains = gain.astype(jnp.float32).reshape(2 * n, 1, half)
    e = jnp.repeat(exps.astype(jnp.float32), HB, axis=1).reshape(steps, blocks, 2 * n, half).transpose(0, 2, 1, 3)
    grid_spec = pltpu.PrefetchScalarGridSpec(
        num_scalar_prefetch=1,
        grid=(steps,),
        in_specs=[pl.BlockSpec((tile, half), lambda i, ids: (i, 0))] * (2 * n)
        + [
            pl.BlockSpec((2 * n, 1, half), lambda i, ids: (0, 0, 0)),
            pl.BlockSpec((1, 2 * n, blocks, half), lambda i, ids: (i, 0, 0, 0)),
            pl.BlockSpec((1, 2 * n, blocks, half), lambda i, ids: (i, 0, 0, 0)),
        ],
        out_specs=pl.BlockSpec((tile, d), lambda i, ids: (i, 0)),
    )
    return pl.pallas_call(
        functools.partial(_norm_kernel, n),
        grid_spec=grid_spec,
        out_shape=jax.ShapeDtypeStruct((rows, d), jnp.bfloat16),
        compiler_params=_params(40),
        cost_estimate=pl.CostEstimate(flops=8 * rows * d, bytes_accessed=4 * rows * d, transcendentals=0),
        name="norm",
    )(ids, *left, *right, gains, jnp.exp2(-e), jnp.exp2(e))


def hadamard_table(order):
    table = jnp.ones((1, 1), dtype=jnp.float32)
    while table.shape[0] < order:
        upper = jnp.concatenate([table, table], axis=1)
        lower = jnp.concatenate([table, -table], axis=1)
        table = jnp.concatenate([upper, lower], axis=0)
    return table


def rotary_tables(positions):
    half = HD // 2
    inv_freq = jnp.exp(-(jnp.arange(half, dtype=jnp.float32) * (2.0 / HD)) * math.log(500000.0))
    angles = positions.astype(jnp.float32)[:, None] * inv_freq[None, :]
    cos, sin = jnp.cos(angles), jnp.sin(angles)
    return jnp.concatenate([cos, cos], axis=1), jnp.concatenate([-sin, sin], axis=1)


def local(
    hidden_in,
    attn_gain,
    query_weight,
    keys,
    values,
    offset,
    out_weight,
    sign_bits,
    attn_exps,
    norm_gain,
    norm_exps,
):
    n_tp, csz, gsz = lax.axis_size("tp"), lax.axis_size("ctx"), lax.axis_size("groups")
    yc = 2 if n_tp % 2 == 0 else 1
    zc = n_tp // yc
    tp, ctx, grp = lax.axis_index("tp"), lax.axis_index("ctx"), lax.axis_index("groups")
    z, y = tp // yc, tp % yc
    rows, width = hidden_in.shape
    d = width * n_tp
    heads = query_weight.shape[1] // HD
    all_heads = heads * n_tp
    depth = out_weight.shape[0]
    cols = d // zc

    column = tp * heads // (all_heads // KVH) * HD
    own_keys = lax.dynamic_slice_in_dim(keys, column, HD, 1)
    own_values = lax.dynamic_slice_in_dim(values, column, HD, 1)
    span = keys.shape[0]
    all_keys = _both(own_keys, "ctx", csz).reshape(csz * span, HD)
    all_values = _both(own_values, "ctx", csz).reshape(csz * span, HD)

    left, right, ids = gather_tp(hidden_in, zc, yc)
    start = (offset[0] + ctx * rows).astype(jnp.int32)
    cos, sin = rotary_tables(start + jnp.arange(rows, dtype=jnp.int32))
    q = project_queries(left, right, ids, attn_gain, query_weight, cos, sin)

    piece = depth // (gsz * csz)
    mine = lax.dynamic_slice_in_dim(out_weight, (grp * csz + ctx) * piece, piece, 0)
    far = []
    for k in range(1, zc):
        block = lax.dynamic_slice_in_dim(mine, (z + k) % zc * cols, cols, 1)
        far.append(_permute(block, "tp", [(s, (s + k * yc) % n_tp) for s in range(n_tp)]))
    far = _both(_both(jnp.stack(far), "groups", gsz), "ctx", csz)

    attended = attend(q, all_keys, all_values, start.reshape(1), span)
    atts = [attended] + [
        _permute(attended, "tp", [(s, (s + k * yc) % n_tp) for s in range(n_tp)]) for k in range(1, zc)
    ]

    tile = 2 * HB
    h = hadamard_table(HB)
    zero = jnp.zeros_like(h)
    table = jnp.concatenate([jnp.concatenate([h, zero], 1), jnp.concatenate([zero, h], 1)], 0).astype(jnp.bfloat16)
    signs = (2 * sign_bits - 1).astype(jnp.bfloat16)
    root = 1.0 / math.sqrt(HB)

    def columns_of(side):
        return (z * yc + side) * width

    def code_half(side, out_type):
        e = lax.dynamic_slice_in_dim(attn_exps, columns_of(side) // HB, width // HB, 1).astype(jnp.float32)
        scale = jnp.repeat(jnp.exp2(-e) * root, HB, axis=1)
        sg = lax.dynamic_slice_in_dim(signs, columns_of(side), width, 0)[:, None]
        return code_terms(atts, out_weight, far, table, sg, scale, z, side, out_type)

    sent = code_half(1 - y, jnp.bfloat16)
    theirs = _permute(sent, "tp", [(s, s ^ 1) for s in range(n_tp)])
    mine_sum = code_half(y, jnp.float32)
    e = lax.dynamic_slice_in_dim(attn_exps, columns_of(y) // HB, width // HB, 1).astype(jnp.float32)
    up = jnp.repeat(jnp.exp2(e) * root, HB, axis=1)
    sg = lax.dynamic_slice_in_dim(signs, columns_of(y), width, 0).astype(jnp.float32)[None, :]
    residual = add_residual(mine_sum, theirs, hidden_in, table, up, sg)

    left, right, ids = gather_tp(residual, zc, yc)
    return norm_rows(left, right, ids, norm_gain, norm_exps)


def solution(mesh):
    return jax.shard_map(
        local,
        mesh=mesh,
        in_specs=(
            P(("groups", "ctx"), "tp"),
            P(),
            P(None, "tp"),
            P(("groups", "ctx"), None),
            P(("groups", "ctx"), None),
            P("groups"),
            P("tp", None),
            P(),
            P(("groups", "ctx"), None),
            P(),
            P(("groups", "ctx"), None),
        ),
        out_specs=P(("groups", "ctx"), None),
        check_vma=False,
    )
```

```python
import functools
import math

import jax
import jax.numpy as jnp
from jax import lax
from jax.experimental import pallas as pl
from jax.experimental.pallas import tpu as pltpu
from jax.sharding import PartitionSpec as P

HD = 128
KVH = 4
HB = 128
RB = 32
MIB = 1 << 20
EPS = 1e-05
LOG2E = math.log2(math.e)


def _params(mib, **kw):
    return pltpu.CompilerParams(vmem_limit_bytes=mib * MIB, **kw)


def _cost(flops, moved):
    return pl.CostEstimate(flops=flops, bytes_accessed=moved, transcendentals=0)


def _permute(value, axis, pairs):
    return lax.ppermute(value, axis, pairs)


def _both(value, axis, count):
    if count == 2:
        other = _permute(value, axis, [(0, 1), (1, 0)])
        first = lax.axis_index(axis) == 0
        return jnp.stack([jnp.where(first, value, other), jnp.where(first, other, value)])
    return lax.all_gather(value, axis, axis=0)


def _spread(blocks, places, axis, count):
    if count == 2:
        mate = [_permute(b, axis, [(0, 1), (1, 0)]) for b in blocks]
        return blocks + mate, [2 * p + lax.axis_index(axis) for p in places] + [
            2 * p + 1 - lax.axis_index(axis) for p in places
        ]
    whole = [lax.all_gather(b, axis, axis=0) for b in blocks]
    return [w[i] for w in whole for i in range(count)], [count * p + i for p in places for i in range(count)]


def _after(values, events):
    return list(lax.optimization_barrier((tuple(values), tuple(events)))[0])


class Line:
    def __init__(self, zc, yc):
        self.zc, self.yc, self.n = zc, yc, zc * yc
        self.z = lax.axis_index("tp") // yc
        self.y = lax.axis_index("tp") % yc

    def across(self, v):
        return _permute(v, "tp", [(s, s ^ 1) for s in range(self.n)])

    def up(self, v, k):
        zc, yc = self.zc, self.yc
        return _permute(v, "tp", [(s, s + yc) for s in range(self.n) if k - 1 <= s // yc < zc - 1])

    def down(self, v, k):
        zc, yc = self.zc, self.yc
        return _permute(v, "tp", [(s, s - yc) for s in range(self.n) if 1 <= s // yc <= zc - k])

    def pick(self, a, b, c, d):
        z = self.z
        return jnp.where(z == 0, a, jnp.where(z == 1, b, jnp.where(z == 2, c, d)))

    def ids(self):
        layers = [self.z, self.pick(1, 0, 1, 2), self.pick(2, 2, 3, 1), self.pick(3, 3, 0, 0)]
        y, yc = self.y, self.yc
        return jnp.stack([l * yc + y for l in layers] + [l * yc + (1 - y) for l in layers]).astype(jnp.int32)

    def gather(self, x):
        z, bar = self.z, lax.optimization_barrier
        y0, u1, d1 = bar((self.across(x), self.up(x, 1), self.down(x, 1)))
        va = jnp.where(z == 0, d1, u1)
        (va, u1, d1), _ = bar(((va, u1, d1), (yield y0)))
        ya, u2, d2 = bar((self.across(va), self.up(u1, 2), self.down(d1, 2)))
        vb = jnp.where(z == 0, d2, jnp.where(z == 3, u2, d1))
        (vb, u2, d2), _ = bar(((vb, u2, d2), (yield ya)))
        yb, u3, d3 = bar((self.across(vb), self.up(u2, 3), self.down(d2, 3)))
        vc = jnp.where(z == 0, d3, jnp.where(z == 1, d2, jnp.where(z == 2, u2, u3)))
        (vc,), _ = bar(((vc,), (yield yb)))
        yield [x, va, vb, vc, y0, ya, yb, self.across(vc)]


def gather_tp(value, zc, yc):
    if zc == 4 and yc == 2:
        line = Line(zc, yc)
        return line.gather(value), line.ids()
    n = zc * yc

    def steps():
        whole = lax.all_gather(value, "tp", axis=0)
        yield whole
        yield whole
        yield whole
        yield [whole[i] for i in range(n)]

    return steps(), jnp.arange(n, dtype=jnp.int32)


def _query_kernel(n, heads, ids, *refs):
    parts = refs[:n]
    gain, weight, cos, sin, out = refs[n:]
    width = parts[0].shape[1]
    d = n * width
    total = None
    for p in parts:
        f = p[...].astype(jnp.float32)
        s = jnp.sum(f * f, axis=1, keepdims=True)
        total = s if total is None else total + s
    r = lax.rsqrt(total / d + EPS)
    acc = None
    for i in range(n):
        at = ids[i]
        normed = (parts[i][...].astype(jnp.float32) * r * gain[at]).astype(jnp.bfloat16)
        rows = pl.ds(pl.multiple_of(at * width, width), width)
        t = jnp.dot(normed, weight[rows, :], preferred_element_type=jnp.float32)
        acc = t if acc is None else acc + t
    for h in range(heads):
        v = acc[:, h * HD : (h + 1) * HD]
        turned = v * cos[...] + pltpu.roll(v, HD // 2, 1) * sin[...]
        out[h] = turned.astype(jnp.bfloat16)


def project_queries(blocks, ids, gain, weight, cos, sin):
    n = len(blocks)
    rows, part = blocks[0].shape
    d, width = weight.shape
    heads = width // HD
    tile = min(256, rows)
    gains = gain.astype(jnp.float32).reshape(n, 1, part)
    grid_spec = pltpu.PrefetchScalarGridSpec(
        num_scalar_prefetch=1,
        grid=(rows // tile,),
        in_specs=[pl.BlockSpec((tile, part), lambda i, ids: (i, 0))] * n
        + [
            pl.BlockSpec((n, 1, part), lambda i, ids: (0, 0, 0)),
            pl.BlockSpec((d, width), lambda i, ids: (0, 0), pipeline_mode=pl.Buffered(1)),
            pl.BlockSpec((tile, HD), lambda i, ids: (i, 0)),
            pl.BlockSpec((tile, HD), lambda i, ids: (i, 0)),
        ],
        out_specs=pl.BlockSpec((heads, tile, HD), lambda i, ids: (0, i, 0)),
    )
    return pl.pallas_call(
        functools.partial(_query_kernel, n, heads),
        grid_spec=grid_spec,
        out_shape=jax.ShapeDtypeStruct((heads, rows, HD), jnp.bfloat16),
        compiler_params=_params(48),
        cost_estimate=_cost(2 * rows * d * width, 2 * (rows * d + d * width)),
        name="query_projection",
    )(ids, *blocks, gains, weight, cos, sin)


CK = 1024


def _attend_kernel(heads, tile, span, info, q_ref, k_ref, v_ref, out, s_ref, m_ref, l_ref, acc_ref):
    step = pl.program_id(0)
    scale = LOG2E / math.sqrt(HD)
    m = heads * tile
    q = q_ref[...].reshape(m, HD)
    first_pos = info[0] + step * tile
    row_pos = first_pos + lax.rem(lax.broadcasted_iota(jnp.int32, (m, CK), 0), tile)

    def scores(base, j, masked):
        keys = k_ref[pl.ds(pl.multiple_of(base + j * CK, CK), CK), :]
        s = lax.dot_general(q, keys, (((1,), (1,)), ((), ())), preferred_element_type=jnp.float32)
        if masked:
            col = base + j * CK + lax.broadcasted_iota(jnp.int32, (m, CK), 1)
            s = jnp.where(col <= row_pos, s, -1e30)
        s_ref[:, pl.ds(pl.multiple_of(j * CK, CK), CK)] = s
        top = m_ref[...]
        for c in range(CK // 128):
            top = jnp.maximum(top, s[:, c * 128 : (c + 1) * 128])
        m_ref[...] = top

    def weigh(base, j, top):
        s = s_ref[:, pl.ds(pl.multiple_of(j * CK, CK), CK)]
        p = jnp.exp2((s - top) * scale)
        total = l_ref[...]
        for c in range(CK // 128):
            total = total + p[:, c * 128 : (c + 1) * 128]
        l_ref[...] = total
        vals = v_ref[pl.ds(pl.multiple_of(base + j * CK, CK), CK), :]
        acc_ref[...] += jnp.dot(p.astype(jnp.bfloat16), vals, preferred_element_type=jnp.float32)

    def block(base, full, count):
        m_ref[...] = jnp.full(m_ref.shape, -1e30, jnp.float32)
        l_ref[...] = jnp.zeros(l_ref.shape, jnp.float32)
        acc_ref[...] = jnp.zeros(acc_ref.shape, jnp.float32)

        def loop(n, f):
            lax.fori_loop(0, n, lambda j, c: (f(j), c)[1], 0)

        loop(full, lambda j: scores(base, j, False))
        if count is not full:
            lax.fori_loop(full, count, lambda j, c: (scores(base, j, True), c)[1], 0)
        top = jnp.max(m_ref[...], axis=1, keepdims=True)
        loop(count, lambda j: weigh(base, j, top))
        return top, jnp.sum(l_ref[...], axis=1, keepdims=True), acc_ref[...]

    chunks = span // CK
    blocks = k_ref.shape[0] // span
    top, total, acc = block(0, chunks, chunks)
    for b in range(1, blocks):
        base = b * span
        full = jnp.clip((first_pos + 1 - base) // CK, 0, chunks)
        count = jnp.clip((first_pos + tile - 1 - base) // CK + 1, 0, chunks)
        top2, total2, acc2 = block(base, full, count)
        new = jnp.maximum(top, top2)
        f1 = jnp.exp2((top - new) * scale)
        f2 = jnp.exp2((top2 - new) * scale)
        acc = f1 * acc + f2 * acc2
        total = f1 * total + f2 * total2
        top = new
    res = (acc / total).astype(jnp.bfloat16)
    for h in range(heads):
        out[:, h * HD : (h + 1) * HD] = res[h * tile : (h + 1) * tile]


def attend(q, keys, values, start, span):
    heads, rows, _ = q.shape
    tile = min(1024 // heads, rows)
    m = heads * tile
    total = keys.shape[0]
    grid_spec = pltpu.PrefetchScalarGridSpec(
        num_scalar_prefetch=1,
        grid=(rows // tile,),
        in_specs=[
            pl.BlockSpec((heads, tile, HD), lambda i, info: (0, i, 0)),
            pl.BlockSpec((total, HD), lambda i, info: (0, 0), pipeline_mode=pl.Buffered(1)),
            pl.BlockSpec((total, HD), lambda i, info: (0, 0), pipeline_mode=pl.Buffered(1)),
        ],
        out_specs=pl.BlockSpec((tile, heads * HD), lambda i, info: (i, 0)),
        scratch_shapes=[
            pltpu.VMEM((m, span), jnp.float32),
            pltpu.VMEM((m, 128), jnp.float32),
            pltpu.VMEM((m, 128), jnp.float32),
            pltpu.VMEM((m, HD), jnp.float32),
        ],
    )
    return pl.pallas_call(
        functools.partial(_attend_kernel, heads, tile, span),
        grid_spec=grid_spec,
        out_shape=jax.ShapeDtypeStruct((rows, heads * HD), jnp.bfloat16),
        compiler_params=_params(48),
        cost_estimate=_cost(4 * heads * rows * total * HD, 4 * total * HD),
        name="attend",
    )(start, q, keys, values)


def _spin(x, table):
    hi = x.astype(jnp.bfloat16)
    lo = (x - hi.astype(jnp.float32)).astype(jnp.bfloat16)
    return jnp.dot(hi, table, preferred_element_type=jnp.float32) + jnp.dot(
        lo, table, preferred_element_type=jnp.float32
    )


def _by_row_block(x, scale):
    blocks = scale.shape[0]
    rows, cols = x.shape
    return (x.reshape(blocks, rows // blocks, cols) * scale[:, None, :]).reshape(rows, cols)


def _code_kernel(zc, pieces, info, *refs):
    atts = refs[:zc]
    own = refs[zc]
    far = refs[zc + 1 : zc + 1 + (zc - 1) * pieces]
    table, sign, scale, out = refs[zc + 1 + (zc - 1) * pieces :]
    spin = table[...] * sign[...]
    piece = far[0].shape[0]
    total = None
    for k in range(zc):
        if k == 0:
            a, w = atts[0][...], own[...]
        else:
            a = jnp.concatenate(
                [atts[k][:, pl.ds(pl.multiple_of(info[2 + p] * piece, piece), piece)] for p in range(pieces)], axis=1
            )
            w = jnp.concatenate([f[...] for f in far[(k - 1) * pieces : k * pieces]], axis=0)
        part = jnp.dot(a, w, preferred_element_type=jnp.float32)
        spun = _spin(part, spin)
        coded = jnp.clip(_by_row_block(spun, scale[...]), -127.0, 127.0)
        coded = coded.astype(jnp.bfloat16).astype(jnp.float32)
        total = coded if total is None else total + coded
    out[...] = total.astype(out.dtype)


def code_terms(atts, own, far, places, table, signs, scale, z, side, out_type):
    zc = len(atts)
    rows, depth = atts[0].shape
    piece, cols = far[0][0].shape
    pieces = len(far[0])
    width = cols // 2
    tile = table.shape[0]
    steps = width // tile
    info = jnp.stack([z * (cols // tile) + side * steps, side * steps] + places).astype(jnp.int32)
    grid_spec = pltpu.PrefetchScalarGridSpec(
        num_scalar_prefetch=1,
        grid=(steps,),
        in_specs=[pl.BlockSpec((rows, depth), lambda j, info: (0, 0), pipeline_mode=pl.Buffered(1))] * zc
        + [pl.BlockSpec((depth, tile), lambda j, info: (0, info[0] + j))]
        + [pl.BlockSpec((piece, tile), lambda j, info: (0, info[1] + j))] * (pieces * len(far))
        + [
            pl.BlockSpec((tile, tile), lambda j, info: (0, 0)),
            pl.BlockSpec((tile, 1), lambda j, info: (j, 0)),
            pl.BlockSpec((scale.shape[0], tile), lambda j, info: (0, j)),
        ],
        out_specs=pl.BlockSpec((rows, tile), lambda j, info: (0, j)),
    )
    return pl.pallas_call(
        functools.partial(_code_kernel, zc, pieces),
        grid_spec=grid_spec,
        out_shape=jax.ShapeDtypeStruct((rows, width), out_type),
        compiler_params=_params(48),
        cost_estimate=_cost(2 * zc * rows * width * (depth + 2 * tile), 2 * zc * depth * width),
        name="code_terms",
    )(info, *atts, own, *[f for fs in far for f in fs], table, signs, scale)


def _residual_kernel(mine, theirs, hidden, table, scale, sign, out):
    summed = mine[...] + theirs[...].astype(jnp.float32)
    tile = table.shape[0]
    for j in range(summed.shape[1] // tile):
        at = slice(j * tile, (j + 1) * tile)
        spun = _spin(summed[:, at], table[...])
        projected = _by_row_block(spun, scale[:, at]) * sign[:, at]
        out[:, at] = (hidden[:, at].astype(jnp.float32) + projected).astype(jnp.bfloat16)


def add_residual(mine, theirs, hidden, table, scale, sign):
    rows, width = mine.shape
    tile = min(256, rows)
    blocks = scale.shape[0] * tile // rows
    return pl.pallas_call(
        _residual_kernel,
        grid=(rows // tile,),
        in_specs=[
            pl.BlockSpec((tile, width), lambda i: (i, 0)),
            pl.BlockSpec((tile, width), lambda i: (i, 0)),
            pl.BlockSpec((tile, width), lambda i: (i, 0)),
            pl.BlockSpec(table.shape, lambda i: (0, 0)),
            pl.BlockSpec((blocks, width), lambda i: (i, 0)),
            pl.BlockSpec((1, width), lambda i: (0, 0)),
        ],
        out_specs=pl.BlockSpec((tile, width), lambda i: (i, 0)),
        out_shape=jax.ShapeDtypeStruct((rows, width), jnp.bfloat16),
        compiler_params=_params(40),
        cost_estimate=_cost(4 * rows * width * table.shape[0], 10 * rows * width),
        name="residual",
    )(mine, theirs, hidden, table, scale, sign)


def _norm_kernel(n, ids, *refs):
    parts = refs[:n]
    gain, up, out = refs[n], refs[n + 1], refs[-1]
    rows, width = parts[0].shape
    d = n * width
    total = None
    for p in parts:
        f = p[...].astype(jnp.float32)
        s = jnp.sum(f * f, axis=1, keepdims=True)
        total = s if total is None else total + s
    r = lax.rsqrt(total / d + EPS)
    blocks = up.shape[2]
    for i in range(n):
        at = ids[i]
        e = up[0, at]
        scaled = parts[i][...].astype(jnp.float32) * r
        code = jnp.clip(_by_row_block(scaled, gain[at] * jnp.exp2(-e)), -127.0, 127.0).astype(jnp.bfloat16)
        value = code.reshape(blocks, rows // blocks, width) * jnp.exp2(e).astype(jnp.bfloat16)[:, None, :]
        out[:, pl.ds(pl.multiple_of(at * width, width), width)] = value.reshape(rows, width)


def norm_rows(blocks, ids, gain, exps, done, first, whole):
    n = len(blocks)
    rows, part = blocks[0].shape
    d = n * part
    tile = 128
    steps = rows // tile
    rb = tile // RB
    gains = gain.astype(jnp.float32).reshape(n, 1, part)
    e = jnp.repeat(exps.astype(jnp.float32), HB, axis=1).reshape(steps, rb, n, part).transpose(0, 2, 1, 3)
    earlier = [] if done is None else [done]
    grid_spec = pltpu.PrefetchScalarGridSpec(
        num_scalar_prefetch=1,
        grid=(steps,),
        in_specs=[pl.BlockSpec((tile, part), lambda i, ids: (i, 0))] * n
        + [
            pl.BlockSpec((n, 1, part), lambda i, ids: (0, 0, 0)),
            pl.BlockSpec((1, n, rb, part), lambda i, ids: (i, 0, 0, 0)),
        ]
        + [pl.BlockSpec(memory_space=pl.ANY)] * len(earlier),
        out_specs=pl.BlockSpec((tile, d), lambda i, ids: (first // tile + i, 0)),
    )
    return pl.pallas_call(
        functools.partial(_norm_kernel, n),
        grid_spec=grid_spec,
        out_shape=jax.ShapeDtypeStruct((whole, d), jnp.bfloat16),
        input_output_aliases={n + 3: 0} if earlier else {},
        compiler_params=_params(60),
        cost_estimate=_cost(8 * rows * d, 4 * rows * d),
        name="norm",
    )(ids, *blocks, gains, e, *earlier)


def hadamard_table(order):
    table = jnp.ones((1, 1), dtype=jnp.float32)
    while table.shape[0] < order:
        upper = jnp.concatenate([table, table], axis=1)
        lower = jnp.concatenate([table, -table], axis=1)
        table = jnp.concatenate([upper, lower], axis=0)
    return table


def rotary_tables(positions):
    half = HD // 2
    inv_freq = jnp.exp(-(jnp.arange(half, dtype=jnp.float32) * (2.0 / HD)) * math.log(500000.0))
    angles = positions.astype(jnp.float32)[:, None] * inv_freq[None, :]
    cos, sin = jnp.cos(angles), jnp.sin(angles)
    return jnp.concatenate([cos, cos], axis=1), jnp.concatenate([-sin, sin], axis=1)


def local(
    hidden_in,
    attn_gain,
    query_weight,
    keys,
    values,
    offset,
    out_weight,
    sign_bits,
    attn_exps,
    norm_gain,
    norm_exps,
):
    n_tp, csz, gsz = lax.axis_size("tp"), lax.axis_size("ctx"), lax.axis_size("groups")
    yc = 2 if n_tp % 2 == 0 else 1
    zc = n_tp // yc
    tp, ctx, grp = lax.axis_index("tp"), lax.axis_index("ctx"), lax.axis_index("groups")
    z, y = tp // yc, tp % yc
    rows, width = hidden_in.shape
    d = width * n_tp
    heads = query_weight.shape[1] // HD
    all_heads = heads * n_tp
    depth = out_weight.shape[0]
    cols = d // zc

    column = tp * heads // (all_heads // KVH) * HD
    own_keys = lax.dynamic_slice_in_dim(keys, column, HD, 1)
    own_values = lax.dynamic_slice_in_dim(values, column, HD, 1)
    span = keys.shape[0]
    all_keys = _both(own_keys, "ctx", csz).reshape(csz * span, HD)
    all_values = _both(own_values, "ctx", csz).reshape(csz * span, HD)

    chunks = 2 if rows % (2 * 256) == 0 else 1
    size = rows // chunks
    blocks_per = size // RB
    start = (offset[0] + ctx * rows).astype(jnp.int32)
    cos, sin = rotary_tables(start + jnp.arange(rows, dtype=jnp.int32))
    mine, shares = out_weight, []
    for axis, count, index in (("groups", gsz, grp), ("ctx", csz, ctx)):
        piece = mine.shape[0] // count
        if piece % 128 == 0:
            mine = lax.dynamic_slice_in_dim(mine, index * piece, piece, 0)
            shares.append((axis, count))
    moved = [lax.dynamic_slice_in_dim(mine, (z + k) % zc * cols, cols, 1) for k in range(1, zc)]

    def move(k, event):
        (block,) = _after([moved[k - 1]], event)
        moved[k - 1] = _permute(block, "tp", [(s, (s + k * yc) % n_tp) for s in range(n_tp)])
        return moved[k - 1]

    def share(k, event):
        arrays, places = _after([moved[k - 1]], event), [jnp.int32(0)]
        for axis, count in shares:
            arrays, places = _spread(arrays, places, axis, count)
        return arrays, places

    parts = [hidden_in[c * size : (c + 1) * size] for c in range(chunks)]
    g0, ids = gather_tp(parts[0], zc, yc)
    a = next(g0)
    b = g0.send(a)
    gathered = []
    if chunks == 2:
        g1, _ = gather_tp(_after([parts[1]], [a])[0], zc, yc)
        e = next(g1)
        c = g0.send(b)
        f = g1.send(e)
        gathered.append(g0.send(c))
        g = g1.send(f)
        move(1, [g])
        gathered.append(g1.send(g))
    else:
        c = g0.send(b)
        gathered.append(g0.send(c))
        move(1, [c])

    tile = 2 * HB
    h = hadamard_table(HB)
    zero = jnp.zeros_like(h)
    table = jnp.concatenate([jnp.concatenate([h, zero], 1), jnp.concatenate([zero, h], 1)], 0).astype(jnp.bfloat16)
    signs = (2 * sign_bits - 1).astype(jnp.bfloat16)
    root = 1.0 / math.sqrt(HB)

    def columns_of(side):
        return (z * yc + side) * width

    def exps_of(side, c):
        e = lax.dynamic_slice_in_dim(attn_exps, columns_of(side) // HB, width // HB, 1)
        return jnp.repeat(e[c * blocks_per : (c + 1) * blocks_per].astype(jnp.float32), HB, axis=1)

    order = [1] + list(range(zc - 1, 1, -1))
    heard, last, far = [], None, [None] * (zc - 1)
    for c in range(chunks):
        at = slice(c * size, (c + 1) * size)
        blocks = gathered[c]
        if c:
            marks = [last]
            for k in order[1:-1]:
                move(k, [moved[order[0] - 1]])
                marks.append(moved[k - 1])
            marks += far[order[0] - 1][0]
            move(order[-1], marks[1:2])
            blocks = _after(blocks, marks)
        q = project_queries(blocks, ids, attn_gain, query_weight, cos[at], sin[at])
        if c == 0:
            far[order[0] - 1] = share(order[0], [q])
        last = attend(q, all_keys, all_values, (start + c * size).reshape(1), span)
        heard.append(
            [last] + [_permute(last, "tp", [(s, (s + k * yc) % n_tp) for s in range(n_tp)]) for k in range(1, zc)]
        )
    if chunks == 1:
        for k in order[1:]:
            move(k, [moved[order[0] - 1]])
    for k in order[1:]:
        far[k - 1] = share(k, [heard[0][0]] if k in order[1:-1] else [last])
    places = far[0][1]
    far = [arrays for arrays, _ in far]

    residuals = []
    for c in range(chunks):
        at = slice(c * size, (c + 1) * size)
        atts = heard[c] if c == chunks - 1 else _after(heard[c], [last])

        def code_half(side, out_type):
            scale = jnp.exp2(-exps_of(side, c)) * root
            sg = lax.dynamic_slice_in_dim(signs, columns_of(side), width, 0)[:, None]
            return code_terms(atts, out_weight, far, places, table, sg, scale, z, side, out_type)

        sent = code_half(1 - y, jnp.bfloat16)
        theirs = _permute(sent, "tp", [(s, s ^ 1) for s in range(n_tp)])
        mine_sum = code_half(y, jnp.float32)
        up = jnp.exp2(exps_of(y, c)) * root
        sg = lax.dynamic_slice_in_dim(signs, columns_of(y), width, 0).astype(jnp.float32)[None, :]
        residuals.append(add_residual(mine_sum, theirs, hidden_in[at], table, up, sg))

    finals = []
    g0, ids = gather_tp(residuals[0], zc, yc)
    a = next(g0)
    if chunks == 2:
        g1, _ = gather_tp(_after([residuals[1]], [a])[0], zc, yc)
        b = g0.send(a)
        e = next(g1)
        c = g0.send(b)
        f = g1.send(e)
        finals.append(g0.send(c))
        g = g1.send(f)
        finals.append(g1.send(g))
    else:
        finals.append(g0.send(g0.send(g0.send(a))))
    out = None
    for c, blocks in enumerate(finals):
        e = norm_exps[c * blocks_per : (c + 1) * blocks_per]
        out = norm_rows(blocks, ids, norm_gain, e, out, c * size, rows)
    return out


def solution(mesh):
    return jax.shard_map(
        local,
        mesh=mesh,
        in_specs=(
            P(("groups", "ctx"), "tp"),
            P(),
            P(None, "tp"),
            P(("groups", "ctx"), None),
            P(("groups", "ctx"), None),
            P("groups"),
            P("tp", None),
            P(),
            P(("groups", "ctx"), None),
            P(),
            P(("groups", "ctx"), None),
        ),
        out_specs=P(("groups", "ctx"), None),
        check_vma=False,
    )
```

```python
import functools
import math

import jax
import jax.numpy as jnp
from jax import lax
from jax.experimental import pallas as pl
from jax.experimental.pallas import tpu as pltpu
from jax.sharding import PartitionSpec as P

HD = 128
KVH = 4
HB = 128
RB = 32
MIB = 1 << 20
EPS = 1e-05
LOG2E = math.log2(math.e)


def _params(mib, **kw):
    return pltpu.CompilerParams(vmem_limit_bytes=mib * MIB, **kw)


def _cost(flops, moved):
    return pl.CostEstimate(flops=flops // 20, bytes_accessed=moved // 20, transcendentals=0)


def _permute(value, axis, pairs):
    return lax.ppermute(value, axis, pairs)


def _both(value, axis, count):
    if count == 2:
        other = _permute(value, axis, [(0, 1), (1, 0)])
        first = lax.axis_index(axis) == 0
        return jnp.stack([jnp.where(first, value, other), jnp.where(first, other, value)])
    return lax.all_gather(value, axis, axis=0)


def _spread(blocks, places, axis, count):
    if count == 2:
        mate = [_permute(b, axis, [(0, 1), (1, 0)]) for b in blocks]
        return blocks + mate, [2 * p + lax.axis_index(axis) for p in places] + [
            2 * p + 1 - lax.axis_index(axis) for p in places
        ]
    whole = [lax.all_gather(b, axis, axis=0) for b in blocks]
    return [w[i] for w in whole for i in range(count)], [count * p + i for p in places for i in range(count)]


def _after(values, events):
    return list(lax.optimization_barrier((tuple(values), tuple(events)))[0])


class Line:
    def __init__(self, zc, yc):
        self.zc, self.yc, self.n = zc, yc, zc * yc
        self.z = lax.axis_index("tp") // yc
        self.y = lax.axis_index("tp") % yc

    def across(self, v):
        return _permute(v, "tp", [(s, s ^ 1) for s in range(self.n)])

    def up(self, v, k):
        zc, yc = self.zc, self.yc
        return _permute(v, "tp", [(s, s + yc) for s in range(self.n) if k - 1 <= s // yc < zc - 1])

    def down(self, v, k):
        zc, yc = self.zc, self.yc
        return _permute(v, "tp", [(s, s - yc) for s in range(self.n) if 1 <= s // yc <= zc - k])

    def pick(self, a, b, c, d):
        z = self.z
        return jnp.where(z == 0, a, jnp.where(z == 1, b, jnp.where(z == 2, c, d)))

    def ids(self):
        layers = [self.z, self.pick(1, 0, 1, 2), self.pick(2, 2, 3, 1), self.pick(3, 3, 0, 0)]
        y, yc = self.y, self.yc
        return jnp.stack([l * yc + y for l in layers] + [l * yc + (1 - y) for l in layers]).astype(jnp.int32)

    def gather(self, x):
        z, bar = self.z, lax.optimization_barrier
        d1, u1, y0 = bar((self.down(x, 1), self.up(x, 1), self.across(x)))
        va = jnp.where(z == 0, d1, u1)
        (va, u1, d1), _ = bar(((va, u1, d1), (yield y0)))
        d2, u2, ya = bar((self.down(d1, 2), self.up(u1, 2), self.across(va)))
        vb = jnp.where(z == 0, d2, jnp.where(z == 3, u2, d1))
        (vb, u2, d2), _ = bar(((vb, u2, d2), (yield ya)))
        d3, u3, yb = bar((self.down(d2, 3), self.up(u2, 3), self.across(vb)))
        vc = jnp.where(z == 0, d3, jnp.where(z == 1, d2, jnp.where(z == 2, u2, u3)))
        (vc,), _ = bar(((vc,), (yield yb)))
        yield [x, va, vb, vc, y0, ya, yb, self.across(vc)]


def gather_tp(value, zc, yc):
    if zc == 4 and yc == 2:
        line = Line(zc, yc)
        return line.gather(value), line.ids()
    n = zc * yc

    def steps():
        whole = lax.all_gather(value, "tp", axis=0)
        yield whole
        yield whole
        yield whole
        yield [whole[i] for i in range(n)]

    return steps(), jnp.arange(n, dtype=jnp.int32)


def _query_kernel(n, heads, ids, *refs):
    parts = refs[:n]
    gain, weight, cos, sin, out = refs[n:]
    width = parts[0].shape[1]
    d = n * width
    total = None
    for p in parts:
        f = p[...].astype(jnp.float32)
        s = jnp.sum(f * f, axis=1, keepdims=True)
        total = s if total is None else total + s
    r = lax.rsqrt(total / d + EPS)
    acc = None
    for i in range(n):
        at = ids[i]
        normed = (parts[i][...].astype(jnp.float32) * r * gain[at]).astype(jnp.bfloat16)
        rows = pl.ds(pl.multiple_of(at * width, width), width)
        t = jnp.dot(normed, weight[rows, :], preferred_element_type=jnp.float32)
        acc = t if acc is None else acc + t
    for h in range(heads):
        v = acc[:, h * HD : (h + 1) * HD]
        turned = v * cos[...] + pltpu.roll(v, HD // 2, 1) * sin[...]
        out[h] = turned.astype(jnp.bfloat16)


def project_queries(blocks, ids, gain, weight, cos, sin):
    n = len(blocks)
    rows, part = blocks[0].shape
    d, width = weight.shape
    heads = width // HD
    tile = min(256, rows)
    gains = gain.astype(jnp.float32).reshape(n, 1, part)
    grid_spec = pltpu.PrefetchScalarGridSpec(
        num_scalar_prefetch=1,
        grid=(rows // tile,),
        in_specs=[pl.BlockSpec((tile, part), lambda i, ids: (i, 0))] * n
        + [
            pl.BlockSpec((n, 1, part), lambda i, ids: (0, 0, 0)),
            pl.BlockSpec((d, width), lambda i, ids: (0, 0), pipeline_mode=pl.Buffered(1)),
            pl.BlockSpec((tile, HD), lambda i, ids: (i, 0)),
            pl.BlockSpec((tile, HD), lambda i, ids: (i, 0)),
        ],
        out_specs=pl.BlockSpec((heads, tile, HD), lambda i, ids: (0, i, 0)),
    )
    return pl.pallas_call(
        functools.partial(_query_kernel, n, heads),
        grid_spec=grid_spec,
        out_shape=jax.ShapeDtypeStruct((heads, rows, HD), jnp.bfloat16),
        compiler_params=_params(48),
        cost_estimate=_cost(2 * rows * d * width, 2 * (rows * d + d * width)),
        name="query_projection",
    )(ids, *blocks, gains, weight, cos, sin)


CK = 1024


def _attend_kernel(heads, tile, span, info, q_ref, k_ref, v_ref, out, s_ref, m_ref, l_ref, acc_ref):
    step = pl.program_id(0)
    scale = LOG2E / math.sqrt(HD)
    m = heads * tile
    q = q_ref[...].reshape(m, HD)
    first_pos = info[0] + step * tile
    row_pos = first_pos + lax.rem(lax.broadcasted_iota(jnp.int32, (m, CK), 0), tile)

    def scores(base, j, masked):
        keys = k_ref[pl.ds(pl.multiple_of(base + j * CK, CK), CK), :]
        s = lax.dot_general(q, keys, (((1,), (1,)), ((), ())), preferred_element_type=jnp.float32)
        if masked:
            col = base + j * CK + lax.broadcasted_iota(jnp.int32, (m, CK), 1)
            s = jnp.where(col <= row_pos, s, -1e30)
        s_ref[:, pl.ds(pl.multiple_of(j * CK, CK), CK)] = s
        top = m_ref[...]
        for c in range(CK // 128):
            top = jnp.maximum(top, s[:, c * 128 : (c + 1) * 128])
        m_ref[...] = top

    def weigh(base, j, top):
        s = s_ref[:, pl.ds(pl.multiple_of(j * CK, CK), CK)]
        p = jnp.exp2((s - top) * scale)
        total = l_ref[...]
        for c in range(CK // 128):
            total = total + p[:, c * 128 : (c + 1) * 128]
        l_ref[...] = total
        vals = v_ref[pl.ds(pl.multiple_of(base + j * CK, CK), CK), :]
        acc_ref[...] += jnp.dot(p.astype(jnp.bfloat16), vals, preferred_element_type=jnp.float32)

    def block(base, full, count):
        m_ref[...] = jnp.full(m_ref.shape, -1e30, jnp.float32)
        l_ref[...] = jnp.zeros(l_ref.shape, jnp.float32)
        acc_ref[...] = jnp.zeros(acc_ref.shape, jnp.float32)

        def loop(n, f):
            lax.fori_loop(0, n, lambda j, c: (f(j), c)[1], 0)

        loop(full, lambda j: scores(base, j, False))
        if count is not full:
            lax.fori_loop(full, count, lambda j, c: (scores(base, j, True), c)[1], 0)
        top = jnp.max(m_ref[...], axis=1, keepdims=True)
        loop(count, lambda j: weigh(base, j, top))
        return top, jnp.sum(l_ref[...], axis=1, keepdims=True), acc_ref[...]

    chunks = span // CK
    blocks = k_ref.shape[0] // span
    top, total, acc = block(0, chunks, chunks)
    for b in range(1, blocks):
        base = b * span
        full = jnp.clip((first_pos + 1 - base) // CK, 0, chunks)
        count = jnp.clip((first_pos + tile - 1 - base) // CK + 1, 0, chunks)
        top2, total2, acc2 = block(base, full, count)
        new = jnp.maximum(top, top2)
        f1 = jnp.exp2((top - new) * scale)
        f2 = jnp.exp2((top2 - new) * scale)
        acc = f1 * acc + f2 * acc2
        total = f1 * total + f2 * total2
        top = new
    res = (acc / total).astype(jnp.bfloat16)
    for h in range(heads):
        out[:, h * HD : (h + 1) * HD] = res[h * tile : (h + 1) * tile]


def attend(q, keys, values, start, span):
    heads, rows, _ = q.shape
    tile = min(1024 // heads, rows)
    m = heads * tile
    total = keys.shape[0]
    grid_spec = pltpu.PrefetchScalarGridSpec(
        num_scalar_prefetch=1,
        grid=(rows // tile,),
        in_specs=[
            pl.BlockSpec((heads, tile, HD), lambda i, info: (0, i, 0)),
            pl.BlockSpec((total, HD), lambda i, info: (0, 0), pipeline_mode=pl.Buffered(1)),
            pl.BlockSpec((total, HD), lambda i, info: (0, 0), pipeline_mode=pl.Buffered(1)),
        ],
        out_specs=pl.BlockSpec((tile, heads * HD), lambda i, info: (i, 0)),
        scratch_shapes=[
            pltpu.VMEM((m, span), jnp.float32),
            pltpu.VMEM((m, 128), jnp.float32),
            pltpu.VMEM((m, 128), jnp.float32),
            pltpu.VMEM((m, HD), jnp.float32),
        ],
    )
    return pl.pallas_call(
        functools.partial(_attend_kernel, heads, tile, span),
        grid_spec=grid_spec,
        out_shape=jax.ShapeDtypeStruct((rows, heads * HD), jnp.bfloat16),
        compiler_params=_params(48),
        cost_estimate=_cost(4 * heads * rows * total * HD, 4 * total * HD),
        name="attend",
    )(start, q, keys, values)


def _spin(x, table):
    hi = x.astype(jnp.bfloat16)
    lo = (x - hi.astype(jnp.float32)).astype(jnp.bfloat16)
    return jnp.dot(hi, table, preferred_element_type=jnp.float32) + jnp.dot(
        lo, table, preferred_element_type=jnp.float32
    )


def _spread_exps(exps, first, width):
    count = exps.shape[1]
    shape = (count, width)
    at = first + lax.broadcasted_iota(jnp.int32, shape, 1) // HB
    pick = jnp.where(lax.broadcasted_iota(jnp.int32, shape, 0) == at, 1.0, 0.0).astype(jnp.bfloat16)
    return jnp.dot(exps.astype(jnp.float32).astype(jnp.bfloat16), pick, preferred_element_type=jnp.float32)


def _signs(bits):
    return (2 * bits - 1).astype(jnp.float32)


def _by_row_block(x, scale):
    blocks = scale.shape[0]
    rows, cols = x.shape
    return (x.reshape(blocks, rows // blocks, cols) * scale[:, None, :]).reshape(rows, cols)


def _code_kernel(zc, pieces, first, blocks, info, *refs):
    atts = refs[:zc]
    own = refs[zc]
    far = refs[zc + 1 : zc + 1 + (zc - 1) * pieces]
    table, bits, exps, out = refs[zc + 1 + (zc - 1) * pieces :]
    tile = table.shape[0]
    sign = _signs(bits[...])
    column = (info[0] + pl.program_id(0)) * (tile // HB)
    scale = jnp.exp2(-_spread_exps(exps[first : first + blocks, :], column, tile)) * (1.0 / math.sqrt(HB))
    piece = far[0].shape[0]
    total = None
    for k in range(zc):
        if k == 0:
            a, w = atts[0][...], own[...]
        else:
            a = jnp.concatenate(
                [atts[k][:, pl.ds(pl.multiple_of(info[2 + p] * piece, piece), piece)] for p in range(pieces)], axis=1
            )
            w = jnp.concatenate([f[...] for f in far[(k - 1) * pieces : k * pieces]], axis=0)
        part = jnp.dot(a, w, preferred_element_type=jnp.float32) * sign
        spun = _spin(part, table[...])
        coded = jnp.clip(_by_row_block(spun, scale), -127.0, 127.0)
        coded = coded.astype(jnp.bfloat16).astype(jnp.float32)
        total = coded if total is None else total + coded
    out[...] = total.astype(out.dtype)


def code_terms(atts, own, far, places, table, bits, exps, chunk, z, side, out_type):
    zc = len(atts)
    rows, depth = atts[0].shape
    piece, cols = far[0][0].shape
    pieces = len(far[0])
    width = cols // 2
    tile = table.shape[0]
    steps = width // tile
    blocks = rows // RB
    info = jnp.stack([z * (cols // tile) + side * steps, side * steps] + places).astype(jnp.int32)
    grid_spec = pltpu.PrefetchScalarGridSpec(
        num_scalar_prefetch=1,
        grid=(steps,),
        in_specs=[pl.BlockSpec((rows, depth), lambda j, info: (0, 0), pipeline_mode=pl.Buffered(1))] * zc
        + [pl.BlockSpec((depth, tile), lambda j, info: (0, info[0] + j))]
        + [pl.BlockSpec((piece, tile), lambda j, info: (0, info[1] + j))] * (pieces * len(far))
        + [
            pl.BlockSpec((tile, tile), lambda j, info: (0, 0)),
            pl.BlockSpec((1, tile), lambda j, info: (0, info[0] + j)),
            pl.BlockSpec(exps.shape, lambda j, info: (0, 0)),
        ],
        out_specs=pl.BlockSpec((rows, tile), lambda j, info: (0, j)),
    )
    return pl.pallas_call(
        functools.partial(_code_kernel, zc, pieces, chunk * blocks, blocks),
        grid_spec=grid_spec,
        out_shape=jax.ShapeDtypeStruct((rows, width), out_type),
        compiler_params=_params(48),
        cost_estimate=_cost(2 * zc * rows * width * (depth + 2 * tile), 2 * zc * depth * width),
        name="code_terms",
    )(info, *atts, own, *[f for fs in far for f in fs], table, bits, exps)


def _residual_kernel(first, blocks, info, mine, theirs, hidden, table, bits, exps, out):
    summed = mine[...] + theirs[...].astype(jnp.float32)
    tile = table.shape[0]
    width = summed.shape[1]
    scale = jnp.exp2(_spread_exps(exps[first : first + blocks, :], info[0] * (width // HB), width))
    scale = scale * (1.0 / math.sqrt(HB))
    sign = _signs(bits[...])
    for j in range(width // tile):
        at = slice(j * tile, (j + 1) * tile)
        spun = _spin(summed[:, at], table[...])
        projected = _by_row_block(spun, scale[:, at]) * sign[:, at]
        out[:, at] = (hidden[:, at].astype(jnp.float32) + projected).astype(jnp.bfloat16)


def add_residual(mine, theirs, hidden, table, bits, exps, chunk, tp):
    rows, width = mine.shape
    blocks = rows // RB
    grid_spec = pltpu.PrefetchScalarGridSpec(
        num_scalar_prefetch=1,
        grid=(1,),
        in_specs=[
            pl.BlockSpec((rows, width), lambda i, info: (0, 0)),
            pl.BlockSpec((rows, width), lambda i, info: (0, 0)),
            pl.BlockSpec((rows, width), lambda i, info: (chunk, 0)),
            pl.BlockSpec(table.shape, lambda i, info: (0, 0)),
            pl.BlockSpec((1, width), lambda i, info: (0, info[0])),
            pl.BlockSpec(exps.shape, lambda i, info: (0, 0)),
        ],
        out_specs=pl.BlockSpec((rows, width), lambda i, info: (0, 0)),
    )
    return pl.pallas_call(
        functools.partial(_residual_kernel, chunk * blocks, blocks),
        grid_spec=grid_spec,
        out_shape=jax.ShapeDtypeStruct((rows, width), jnp.bfloat16),
        compiler_params=_params(48),
        cost_estimate=_cost(4 * rows * width * table.shape[0], 10 * rows * width),
        name="residual",
    )(tp.astype(jnp.int32).reshape(1), mine, theirs, hidden, table, bits, exps)


def _norm_kernel(n, ids, *refs):
    parts = refs[:n]
    gain, exps, out = refs[n], refs[n + 1], refs[-1]
    rows, width = parts[0].shape
    d = n * width
    total = None
    for p in parts:
        f = p[...].astype(jnp.float32)
        s = jnp.sum(f * f, axis=1, keepdims=True)
        total = s if total is None else total + s
    r = lax.rsqrt(total / d + EPS)
    blocks = exps.shape[1]
    for i in range(n):
        at = ids[i]
        columns = pl.ds(pl.multiple_of(at * width, width), width)
        e = _spread_exps(exps[0], at * (width // HB), width)
        scaled = parts[i][...].astype(jnp.float32) * r
        g = gain[:, columns].astype(jnp.float32) * jnp.exp2(-e)
        code = jnp.clip(_by_row_block(scaled, g), -127.0, 127.0).astype(jnp.bfloat16)
        value = code.reshape(blocks, rows // blocks, width) * jnp.exp2(e).astype(jnp.bfloat16)[:, None, :]
        out[:, columns] = value.reshape(rows, width)


def norm_rows(blocks, ids, gain, exps, done, chunk, whole):
    n = len(blocks)
    rows, part = blocks[0].shape
    d = n * part
    tile = 128
    steps = rows // tile
    rb = tile // RB
    earlier = [] if done is None else [done]
    grid_spec = pltpu.PrefetchScalarGridSpec(
        num_scalar_prefetch=1,
        grid=(steps,),
        in_specs=[pl.BlockSpec((tile, part), lambda i, ids: (i, 0))] * n
        + [
            pl.BlockSpec((1, d), lambda i, ids: (0, 0)),
            pl.BlockSpec((1, rb, exps.shape[1]), lambda i, ids: (chunk * steps + i, 0, 0)),
        ]
        + [pl.BlockSpec(memory_space=pl.ANY)] * len(earlier),
        out_specs=pl.BlockSpec((tile, d), lambda i, ids: (chunk * steps + i, 0)),
    )
    return pl.pallas_call(
        functools.partial(_norm_kernel, n),
        grid_spec=grid_spec,
        out_shape=jax.ShapeDtypeStruct((whole, d), jnp.bfloat16),
        input_output_aliases={n + 3: 0} if earlier else {},
        compiler_params=_params(60),
        cost_estimate=_cost(8 * rows * d, 4 * rows * d),
        name="norm",
    )(ids, *blocks, gain, exps.reshape(-1, rb, exps.shape[1]), *earlier)


def hadamard_table(order):
    table = jnp.ones((1, 1), dtype=jnp.float32)
    while table.shape[0] < order:
        upper = jnp.concatenate([table, table], axis=1)
        lower = jnp.concatenate([table, -table], axis=1)
        table = jnp.concatenate([upper, lower], axis=0)
    return table


def rotary_tables(positions):
    half = HD // 2
    inv_freq = jnp.exp(-(jnp.arange(half, dtype=jnp.float32) * (2.0 / HD)) * math.log(500000.0))
    angles = positions.astype(jnp.float32)[:, None] * inv_freq[None, :]
    cos, sin = jnp.cos(angles), jnp.sin(angles)
    return jnp.concatenate([cos, cos], axis=1), jnp.concatenate([-sin, sin], axis=1)


def local(
    hidden_in,
    attn_gain,
    query_weight,
    keys,
    values,
    offset,
    out_weight,
    sign_bits,
    attn_exps,
    norm_gain,
    norm_exps,
):
    n_tp, csz, gsz = lax.axis_size("tp"), lax.axis_size("ctx"), lax.axis_size("groups")
    yc = 2 if n_tp % 2 == 0 else 1
    zc = n_tp // yc
    tp, ctx, grp = lax.axis_index("tp"), lax.axis_index("ctx"), lax.axis_index("groups")
    z, y = tp // yc, tp % yc
    rows, width = hidden_in.shape
    d = width * n_tp
    heads = query_weight.shape[1] // HD
    all_heads = heads * n_tp
    depth = out_weight.shape[0]
    cols = d // zc

    column = tp * heads // (all_heads // KVH) * HD
    own_keys = lax.dynamic_slice_in_dim(keys, column, HD, 1)
    own_values = lax.dynamic_slice_in_dim(values, column, HD, 1)
    span = keys.shape[0]
    all_keys = _both(own_keys, "ctx", csz).reshape(csz * span, HD)
    all_values = _both(own_values, "ctx", csz).reshape(csz * span, HD)

    size = rows // 2
    blocks_per = size // RB
    halves = [slice(0, size), slice(size, rows)]
    start = (offset[0] + ctx * rows).astype(jnp.int32)
    cos, sin = rotary_tables(start + jnp.arange(rows, dtype=jnp.int32))

    mine, shares = out_weight, []
    for axis, count, index in (("groups", gsz, grp), ("ctx", csz, ctx)):
        piece = mine.shape[0] // count
        if piece % 128 == 0:
            mine = lax.dynamic_slice_in_dim(mine, index * piece, piece, 0)
            shares.append((axis, count))
    steps = list(range(1, zc))
    batches = [steps[1::3], steps[2::3], steps[0::3]]
    moved, far = {}, {}

    def move(batch, *event):
        pieces = [lax.dynamic_slice_in_dim(mine, (z + k) % zc * cols, cols, 1) for k in batch]
        for k, piece in zip(batch, _after(pieces, event)):
            moved[k] = _permute(piece, "tp", [(s, (s + k * yc) % n_tp) for s in range(n_tp)])
            far[k] = [moved[k]], [jnp.int32(0)]

    def share(batch, level, *event):
        if level < len(shares):
            for k in batch:
                arrays, places = far[k]
                far[k] = _spread(_after(arrays, event), places, *shares[level])

    def arrived(batch):
        return [a for k in batch for a in far[k][0]]

    g0, ids = gather_tp(hidden_in[halves[0]], zc, yc)
    a1 = next(g0)
    g1, _ = gather_tp(_after([hidden_in[halves[1]]], [a1])[0], zc, yc)
    a2 = g0.send(a1)
    b1 = next(g1)
    a3 = g0.send(a2)
    b2 = g1.send(b1)
    move(batches[0], a3, b2)
    first = g0.send(a3)
    b3 = g1.send(b2)
    event = [b3] + arrived(batches[0])
    move(batches[1], *event)
    share(batches[0], 0, *event)
    second = g1.send(event)

    def queries_of(c, blocks):
        return project_queries(blocks, ids, attn_gain, query_weight, cos[halves[c]], sin[halves[c]])

    def heard_by(c, q):
        own = attend(q, all_keys, all_values, (start + c * size).reshape(1), span)
        return [own] + [_permute(own, "tp", [(s, (s + k * yc) % n_tp) for s in range(n_tp)]) for k in range(1, zc)]

    q = queries_of(0, first)
    move(batches[2], q)
    heard = [heard_by(0, q)]
    done = heard[0][0]
    share(batches[1], 0, done)
    share(batches[0], 1, done)
    q = queries_of(1, _after(second, [done]))
    share(batches[2], 0, q)
    heard.append(heard_by(1, q))
    done = heard[1][0]
    share(batches[1], 1, done)
    share(batches[2], 1, done)
    heard[0] = _after(heard[0], [done])
    places = far[1][1]
    far = [far[k][0] for k in steps]

    tile = 2 * HB
    h = hadamard_table(HB)
    zero = jnp.zeros_like(h)
    table = jnp.concatenate([jnp.concatenate([h, zero], 1), jnp.concatenate([zero, h], 1)], 0).astype(jnp.bfloat16)
    bits = sign_bits.reshape(1, d)

    def code_half(c, side, out_type):
        return code_terms(heard[c], out_weight, far, places, table, bits, attn_exps, c, z, side, out_type)

    residuals = []
    for c in range(2):
        sent = code_half(c, 1 - y, jnp.bfloat16)
        theirs = _permute(sent, "tp", [(s, s ^ 1) for s in range(n_tp)])
        mine_sum = code_half(c, y, jnp.float32)
        residuals.append(add_residual(mine_sum, theirs, hidden_in, table, bits, attn_exps, c, tp))
        if c == 0:
            heard[1] = _after(heard[1], residuals)

    g0, ids = gather_tp(residuals[0], zc, yc)
    a1 = next(g0)
    g1, _ = gather_tp(_after([residuals[1]], [a1])[0], zc, yc)
    a2 = g0.send(a1)
    b1 = next(g1)
    a3 = g0.send(a2)
    b2 = g1.send(b1)
    first = g0.send(a3)
    b3 = g1.send(b2)
    second = g1.send(b3)
    norm_row = norm_gain.reshape(1, d)
    out = norm_rows(first, ids, norm_row, norm_exps, None, 0, rows)
    return norm_rows(second, ids, norm_row, norm_exps, out, 1, rows)


def solution(mesh):
    return jax.shard_map(
        local,
        mesh=mesh,
        in_specs=(
            P(("groups", "ctx"), "tp"),
            P(),
            P(None, "tp"),
            P(("groups", "ctx"), None),
            P(("groups", "ctx"), None),
            P("groups"),
            P("tp", None),
            P(),
            P(("groups", "ctx"), None),
            P(),
            P(("groups", "ctx"), None),
        ),
        out_specs=P(("groups", "ctx"), None),
        check_vma=False,
    )
```

```python
import functools
import math

import jax
import jax.numpy as jnp
from jax import lax
from jax.experimental import pallas as pl
from jax.experimental.pallas import tpu as pltpu
from jax.sharding import PartitionSpec as P

HD = 128
KVH = 4
HB = 128
RB = 32
MIB = 1 << 20
EPS = 1e-05
LOG2E = math.log2(math.e)


def _params(mib, **kw):
    return pltpu.CompilerParams(vmem_limit_bytes=mib * MIB, **kw)


def _cost(flops, moved):
    return pl.CostEstimate(flops=flops // 20, bytes_accessed=moved // 20, transcendentals=0)


def _permute(value, axis, pairs):
    return lax.ppermute(value, axis, pairs)


def _both(value, axis, count):
    if count == 2:
        other = _permute(value, axis, [(0, 1), (1, 0)])
        first = lax.axis_index(axis) == 0
        return jnp.stack([jnp.where(first, value, other), jnp.where(first, other, value)])
    return lax.all_gather(value, axis, axis=0)


def _spread(blocks, places, axis, count):
    if count == 2:
        mate = [_permute(b, axis, [(0, 1), (1, 0)]) for b in blocks]
        return blocks + mate, [2 * p + lax.axis_index(axis) for p in places] + [
            2 * p + 1 - lax.axis_index(axis) for p in places
        ]
    whole = [lax.all_gather(b, axis, axis=0) for b in blocks]
    return [w[i] for w in whole for i in range(count)], [count * p + i for p in places for i in range(count)]


def _after(values, events):
    return list(lax.optimization_barrier((tuple(values), tuple(events)))[0])


class Line:
    def __init__(self, zc, yc):
        self.zc, self.yc, self.n = zc, yc, zc * yc
        self.z = lax.axis_index("tp") // yc
        self.y = lax.axis_index("tp") % yc

    def across(self, v):
        return _permute(v, "tp", [(s, s ^ 1) for s in range(self.n)])

    def up(self, v, k):
        zc, yc = self.zc, self.yc
        return _permute(v, "tp", [(s, s + yc) for s in range(self.n) if k - 1 <= s // yc < zc - 1])

    def down(self, v, k):
        zc, yc = self.zc, self.yc
        return _permute(v, "tp", [(s, s - yc) for s in range(self.n) if 1 <= s // yc <= zc - k])

    def pick(self, a, b, c, d):
        z = self.z
        return jnp.where(z == 0, a, jnp.where(z == 1, b, jnp.where(z == 2, c, d)))

    def ids(self):
        layers = [self.z, self.pick(1, 0, 1, 2), self.pick(2, 2, 3, 1), self.pick(3, 3, 0, 0)]
        y, yc = self.y, self.yc
        return jnp.stack([l * yc + y for l in layers] + [l * yc + (1 - y) for l in layers]).astype(jnp.int32)

    def gather(self, x):
        z, bar = self.z, lax.optimization_barrier
        d1, u1, y0 = bar((self.down(x, 1), self.up(x, 1), self.across(x)))
        va = jnp.where(z == 0, d1, u1)
        (va, u1, d1), _ = bar(((va, u1, d1), (yield y0)))
        d2, u2, ya = bar((self.down(d1, 2), self.up(u1, 2), self.across(va)))
        vb = jnp.where(z == 0, d2, jnp.where(z == 3, u2, d1))
        (vb, u2, d2), _ = bar(((vb, u2, d2), (yield ya)))
        d3, u3, yb = bar((self.down(d2, 3), self.up(u2, 3), self.across(vb)))
        vc = jnp.where(z == 0, d3, jnp.where(z == 1, d2, jnp.where(z == 2, u2, u3)))
        (vc,), _ = bar(((vc,), (yield yb)))
        yield [x, va, vb, vc, y0, ya, yb, self.across(vc)]


def gather_tp(value, zc, yc):
    if zc == 4 and yc == 2:
        line = Line(zc, yc)
        return line.gather(value), line.ids()
    n = zc * yc

    def steps():
        whole = lax.all_gather(value, "tp", axis=0)
        yield whole
        yield whole
        yield whole
        yield [whole[i] for i in range(n)]

    return steps(), jnp.arange(n, dtype=jnp.int32)


def _squares(parts):
    total = None
    for p in parts:
        for c in range(0, p.shape[1], 128):
            f = p[:, c : c + 128].astype(jnp.float32)
            total = f * f if total is None else total + f * f
    return jnp.sum(total, axis=1, keepdims=True)


def _query_kernel(n, heads, ids, *refs):
    parts = refs[:n]
    gain, weight, cos, sin, out = refs[n:]
    width = parts[0].shape[1]
    d = n * width
    r = lax.rsqrt(_squares([p[...] for p in parts]) / d + EPS)
    acc = None
    for i in range(n):
        at = ids[i]
        normed = (parts[i][...].astype(jnp.float32) * r * gain[at]).astype(jnp.bfloat16)
        rows = pl.ds(pl.multiple_of(at * width, width), width)
        t = jnp.dot(normed, weight[rows, :], preferred_element_type=jnp.float32)
        acc = t if acc is None else acc + t
    for h in range(heads):
        v = acc[:, h * HD : (h + 1) * HD]
        turned = v * cos[...] + pltpu.roll(v, HD // 2, 1) * sin[...]
        out[h] = turned.astype(jnp.bfloat16)


def project_queries(blocks, ids, gain, weight, cos, sin):
    n = len(blocks)
    rows, part = blocks[0].shape
    d, width = weight.shape
    heads = width // HD
    tile = min(256, rows)
    gains = gain.astype(jnp.float32).reshape(n, 1, part)
    grid_spec = pltpu.PrefetchScalarGridSpec(
        num_scalar_prefetch=1,
        grid=(rows // tile,),
        in_specs=[pl.BlockSpec((tile, part), lambda i, ids: (i, 0))] * n
        + [
            pl.BlockSpec((n, 1, part), lambda i, ids: (0, 0, 0)),
            pl.BlockSpec((d, width), lambda i, ids: (0, 0), pipeline_mode=pl.Buffered(1)),
            pl.BlockSpec((tile, HD), lambda i, ids: (i, 0)),
            pl.BlockSpec((tile, HD), lambda i, ids: (i, 0)),
        ],
        out_specs=pl.BlockSpec((heads, tile, HD), lambda i, ids: (0, i, 0)),
    )
    return pl.pallas_call(
        functools.partial(_query_kernel, n, heads),
        grid_spec=grid_spec,
        out_shape=jax.ShapeDtypeStruct((heads, rows, HD), jnp.bfloat16),
        compiler_params=_params(48),
        cost_estimate=_cost(2 * rows * d * width, 2 * (rows * d + d * width)),
        name="query_projection",
    )(ids, *blocks, gains, weight, cos, sin)


CK = 1024


def _attend_kernel(heads, tile, span, info, q_ref, k_ref, v_ref, out, s_ref, m_ref, l_ref, acc_ref):
    step = pl.program_id(0)
    scale = LOG2E / math.sqrt(HD)
    m = heads * tile
    q = q_ref[...].reshape(m, HD)
    first_pos = info[0] + step * tile
    row_pos = first_pos + lax.rem(lax.broadcasted_iota(jnp.int32, (m, CK), 0), tile)

    def scores(base, j, masked):
        keys = k_ref[pl.ds(pl.multiple_of(base + j * CK, CK), CK), :]
        s = lax.dot_general(q, keys, (((1,), (1,)), ((), ())), preferred_element_type=jnp.float32)
        if masked:
            col = base + j * CK + lax.broadcasted_iota(jnp.int32, (m, CK), 1)
            s = jnp.where(col <= row_pos, s, -1e30)
        s_ref[:, pl.ds(pl.multiple_of(j * CK, CK), CK)] = s
        top = m_ref[...]
        for c in range(CK // 128):
            top = jnp.maximum(top, s[:, c * 128 : (c + 1) * 128])
        m_ref[...] = top

    def weigh(base, j, top):
        s = s_ref[:, pl.ds(pl.multiple_of(j * CK, CK), CK)]
        p = jnp.exp2((s - top) * scale)
        total = l_ref[...]
        for c in range(CK // 128):
            total = total + p[:, c * 128 : (c + 1) * 128]
        l_ref[...] = total
        vals = v_ref[pl.ds(pl.multiple_of(base + j * CK, CK), CK), :]
        acc_ref[...] += jnp.dot(p.astype(jnp.bfloat16), vals, preferred_element_type=jnp.float32)

    def block(base, full, count):
        m_ref[...] = jnp.full(m_ref.shape, -1e30, jnp.float32)
        l_ref[...] = jnp.zeros(l_ref.shape, jnp.float32)
        acc_ref[...] = jnp.zeros(acc_ref.shape, jnp.float32)

        def loop(n, f):
            lax.fori_loop(0, n, lambda j, c: (f(j), c)[1], 0)

        loop(full, lambda j: scores(base, j, False))
        if count is not full:
            lax.fori_loop(full, count, lambda j, c: (scores(base, j, True), c)[1], 0)
        top = jnp.max(m_ref[...], axis=1, keepdims=True)
        loop(count, lambda j: weigh(base, j, top))
        return top, jnp.sum(l_ref[...], axis=1, keepdims=True), acc_ref[...]

    chunks = span // CK
    blocks = k_ref.shape[0] // span
    top, total, acc = block(0, chunks, chunks)
    for b in range(1, blocks):
        base = b * span
        full = jnp.clip((first_pos + 1 - base) // CK, 0, chunks)
        count = jnp.clip((first_pos + tile - 1 - base) // CK + 1, 0, chunks)
        top2, total2, acc2 = block(base, full, count)
        new = jnp.maximum(top, top2)
        f1 = jnp.exp2((top - new) * scale)
        f2 = jnp.exp2((top2 - new) * scale)
        acc = f1 * acc + f2 * acc2
        total = f1 * total + f2 * total2
        top = new
    res = (acc / total).astype(jnp.bfloat16)
    for h in range(heads):
        out[:, h * HD : (h + 1) * HD] = res[h * tile : (h + 1) * tile]


def attend(q, keys, values, start, span):
    heads, rows, _ = q.shape
    tile = min(1024 // heads, rows)
    m = heads * tile
    total = keys.shape[0]
    grid_spec = pltpu.PrefetchScalarGridSpec(
        num_scalar_prefetch=1,
        grid=(rows // tile,),
        in_specs=[
            pl.BlockSpec((heads, tile, HD), lambda i, info: (0, i, 0)),
            pl.BlockSpec((total, HD), lambda i, info: (0, 0), pipeline_mode=pl.Buffered(1)),
            pl.BlockSpec((total, HD), lambda i, info: (0, 0), pipeline_mode=pl.Buffered(1)),
        ],
        out_specs=pl.BlockSpec((tile, heads * HD), lambda i, info: (i, 0)),
        scratch_shapes=[
            pltpu.VMEM((m, span), jnp.float32),
            pltpu.VMEM((m, 128), jnp.float32),
            pltpu.VMEM((m, 128), jnp.float32),
            pltpu.VMEM((m, HD), jnp.float32),
        ],
    )
    return pl.pallas_call(
        functools.partial(_attend_kernel, heads, tile, span),
        grid_spec=grid_spec,
        out_shape=jax.ShapeDtypeStruct((rows, heads * HD), jnp.bfloat16),
        compiler_params=_params(48),
        cost_estimate=_cost(4 * heads * rows * total * HD, 4 * total * HD),
        name="attend",
    )(start, q, keys, values)


def _spin(x, table):
    hi = x.astype(jnp.bfloat16)
    lo = (x - hi.astype(jnp.float32)).astype(jnp.bfloat16)
    return jnp.dot(hi, table, preferred_element_type=jnp.float32) + jnp.dot(
        lo, table, preferred_element_type=jnp.float32
    )


def _spread_exps(exps, first, width):
    count = exps.shape[1]
    shape = (count, width)
    at = first + lax.broadcasted_iota(jnp.int32, shape, 1) // HB
    pick = jnp.where(lax.broadcasted_iota(jnp.int32, shape, 0) == at, 1.0, 0.0).astype(jnp.bfloat16)
    return jnp.dot(exps.astype(jnp.float32).astype(jnp.bfloat16), pick, preferred_element_type=jnp.float32)


def _signs(bits):
    return (2 * bits - 1).astype(jnp.float32)


def _by_row_block(x, scale):
    blocks = scale.shape[0]
    rows, cols = x.shape
    return (x.reshape(blocks, rows // blocks, cols) * scale[:, None, :]).reshape(rows, cols)


def _code_kernel(zc, pieces, first, blocks, info, *refs):
    atts = refs[:zc]
    own = refs[zc]
    far = refs[zc + 1 : zc + 1 + (zc - 1) * pieces]
    table, bits, exps, out = refs[zc + 1 + (zc - 1) * pieces :]
    tile = table.shape[0]
    sign = _signs(bits[...])
    column = (info[0] + pl.program_id(0)) * (tile // HB)
    scale = jnp.exp2(-_spread_exps(exps[first : first + blocks, :], column, tile)) * (1.0 / math.sqrt(HB))
    piece = far[0].shape[0]
    parts = []
    for k in range(zc):
        if k == 0:
            a, w = atts[0][...], own[...]
        else:
            a = jnp.concatenate(
                [atts[k][:, pl.ds(pl.multiple_of(info[2 + p] * piece, piece), piece)] for p in range(pieces)], axis=1
            )
            w = jnp.concatenate([f[...] for f in far[(k - 1) * pieces : k * pieces]], axis=0)
        parts.append(jnp.dot(a, w, preferred_element_type=jnp.float32) * sign)
    rows = parts[0].shape[0]
    spun = _spin(jnp.concatenate(parts, axis=0), table[...])
    total = None
    for k in range(zc):
        coded = jnp.clip(_by_row_block(spun[k * rows : (k + 1) * rows], scale), -127.0, 127.0)
        coded = coded.astype(jnp.bfloat16).astype(jnp.float32)
        total = coded if total is None else total + coded
    out[...] = total.astype(out.dtype)


def code_terms(atts, own, far, places, table, bits, exps, chunk, z, side, out_type):
    zc = len(atts)
    rows, depth = atts[0].shape
    piece, cols = far[0][0].shape
    pieces = len(far[0])
    width = cols // 2
    tile = table.shape[0]
    steps = width // tile
    blocks = rows // RB
    info = jnp.stack([z * (cols // tile) + side * steps, side * steps] + places).astype(jnp.int32)
    grid_spec = pltpu.PrefetchScalarGridSpec(
        num_scalar_prefetch=1,
        grid=(steps,),
        in_specs=[pl.BlockSpec((rows, depth), lambda j, info: (0, 0), pipeline_mode=pl.Buffered(1))] * zc
        + [pl.BlockSpec((depth, tile), lambda j, info: (0, info[0] + j))]
        + [pl.BlockSpec((piece, tile), lambda j, info: (0, info[1] + j))] * (pieces * len(far))
        + [
            pl.BlockSpec((tile, tile), lambda j, info: (0, 0)),
            pl.BlockSpec((1, tile), lambda j, info: (0, info[0] + j)),
            pl.BlockSpec(exps.shape, lambda j, info: (0, 0)),
        ],
        out_specs=pl.BlockSpec((rows, tile), lambda j, info: (0, j)),
    )
    return pl.pallas_call(
        functools.partial(_code_kernel, zc, pieces, chunk * blocks, blocks),
        grid_spec=grid_spec,
        out_shape=jax.ShapeDtypeStruct((rows, width), out_type),
        compiler_params=_params(48),
        cost_estimate=_cost(2 * zc * rows * width * (depth + 2 * tile), 2 * zc * depth * width),
        name="code_terms",
    )(info, *atts, own, *[f for fs in far for f in fs], table, bits, exps)


def _residual_kernel(first, blocks, info, mine, theirs, hidden, table, bits, exps, out):
    summed = mine[...] + theirs[...].astype(jnp.float32)
    tile = table.shape[0]
    width = summed.shape[1]
    scale = jnp.exp2(_spread_exps(exps[first : first + blocks, :], info[0] * (width // HB), width))
    scale = scale * (1.0 / math.sqrt(HB))
    sign = _signs(bits[...])
    for j in range(width // tile):
        at = slice(j * tile, (j + 1) * tile)
        spun = _spin(summed[:, at], table[...])
        projected = _by_row_block(spun, scale[:, at]) * sign[:, at]
        out[:, at] = (hidden[:, at].astype(jnp.float32) + projected).astype(jnp.bfloat16)


def add_residual(mine, theirs, hidden, table, bits, exps, chunk, tp):
    rows, width = mine.shape
    blocks = rows // RB
    grid_spec = pltpu.PrefetchScalarGridSpec(
        num_scalar_prefetch=1,
        grid=(1,),
        in_specs=[
            pl.BlockSpec((rows, width), lambda i, info: (0, 0)),
            pl.BlockSpec((rows, width), lambda i, info: (0, 0)),
            pl.BlockSpec((rows, width), lambda i, info: (chunk, 0)),
            pl.BlockSpec(table.shape, lambda i, info: (0, 0)),
            pl.BlockSpec((1, width), lambda i, info: (0, info[0])),
            pl.BlockSpec(exps.shape, lambda i, info: (0, 0)),
        ],
        out_specs=pl.BlockSpec((rows, width), lambda i, info: (0, 0)),
    )
    return pl.pallas_call(
        functools.partial(_residual_kernel, chunk * blocks, blocks),
        grid_spec=grid_spec,
        out_shape=jax.ShapeDtypeStruct((rows, width), jnp.bfloat16),
        compiler_params=_params(48),
        cost_estimate=_cost(4 * rows * width * table.shape[0], 10 * rows * width),
        name="residual",
    )(tp.astype(jnp.int32).reshape(1), mine, theirs, hidden, table, bits, exps)


def _norm_kernel(n, ids, *refs):
    parts = refs[:n]
    gain, exps, out = refs[n], refs[n + 1], refs[-1]
    rows, width = parts[0].shape
    d = n * width
    r = lax.rsqrt(_squares([p[...] for p in parts]) / d + EPS)
    blocks = exps.shape[1]
    for i in range(n):
        at = ids[i]
        columns = pl.ds(pl.multiple_of(at * width, width), width)
        e = _spread_exps(exps[0], at * (width // HB), width)
        scaled = parts[i][...].astype(jnp.float32) * r
        g = gain[:, columns].astype(jnp.float32) * jnp.exp2(-e)
        code = jnp.clip(_by_row_block(scaled, g), -127.0, 127.0).astype(jnp.bfloat16)
        value = code.reshape(blocks, rows // blocks, width) * jnp.exp2(e).astype(jnp.bfloat16)[:, None, :]
        out[:, columns] = value.reshape(rows, width)


def norm_rows(blocks, ids, gain, exps, done, chunk, whole):
    n = len(blocks)
    rows, part = blocks[0].shape
    d = n * part
    tile = 128
    steps = rows // tile
    rb = tile // RB
    earlier = [] if done is None else [done]
    grid_spec = pltpu.PrefetchScalarGridSpec(
        num_scalar_prefetch=1,
        grid=(steps,),
        in_specs=[pl.BlockSpec((tile, part), lambda i, ids: (i, 0))] * n
        + [
            pl.BlockSpec((1, d), lambda i, ids: (0, 0)),
            pl.BlockSpec((1, rb, exps.shape[1]), lambda i, ids: (chunk * steps + i, 0, 0)),
        ]
        + [pl.BlockSpec(memory_space=pl.ANY)] * len(earlier),
        out_specs=pl.BlockSpec((tile, d), lambda i, ids: (chunk * steps + i, 0)),
    )
    return pl.pallas_call(
        functools.partial(_norm_kernel, n),
        grid_spec=grid_spec,
        out_shape=jax.ShapeDtypeStruct((whole, d), jnp.bfloat16),
        input_output_aliases={n + 3: 0} if earlier else {},
        compiler_params=_params(60),
        cost_estimate=_cost(8 * rows * d, 4 * rows * d),
        name="norm",
    )(ids, *blocks, gain, exps.reshape(-1, rb, exps.shape[1]), *earlier)


def hadamard_table(order):
    table = jnp.ones((1, 1), dtype=jnp.float32)
    while table.shape[0] < order:
        upper = jnp.concatenate([table, table], axis=1)
        lower = jnp.concatenate([table, -table], axis=1)
        table = jnp.concatenate([upper, lower], axis=0)
    return table


def rotary_tables(positions):
    half = HD // 2
    inv_freq = jnp.exp(-(jnp.arange(half, dtype=jnp.float32) * (2.0 / HD)) * math.log(500000.0))
    angles = positions.astype(jnp.float32)[:, None] * inv_freq[None, :]
    cos, sin = jnp.cos(angles), jnp.sin(angles)
    return jnp.concatenate([cos, cos], axis=1), jnp.concatenate([-sin, sin], axis=1)


def local(
    hidden_in,
    attn_gain,
    query_weight,
    keys,
    values,
    offset,
    out_weight,
    sign_bits,
    attn_exps,
    norm_gain,
    norm_exps,
):
    n_tp, csz, gsz = lax.axis_size("tp"), lax.axis_size("ctx"), lax.axis_size("groups")
    yc = 2 if n_tp % 2 == 0 else 1
    zc = n_tp // yc
    tp, ctx, grp = lax.axis_index("tp"), lax.axis_index("ctx"), lax.axis_index("groups")
    z, y = tp // yc, tp % yc
    rows, width = hidden_in.shape
    d = width * n_tp
    heads = query_weight.shape[1] // HD
    all_heads = heads * n_tp
    depth = out_weight.shape[0]
    cols = d // zc

    column = tp * heads // (all_heads // KVH) * HD
    own_keys = lax.dynamic_slice_in_dim(keys, column, HD, 1)
    own_values = lax.dynamic_slice_in_dim(values, column, HD, 1)
    span = keys.shape[0]
    all_keys = _both(own_keys, "ctx", csz).reshape(csz * span, HD)
    all_values = _both(own_values, "ctx", csz).reshape(csz * span, HD)

    size = rows // 2
    blocks_per = size // RB
    halves = [slice(0, size), slice(size, rows)]
    start = (offset[0] + ctx * rows).astype(jnp.int32)
    cos, sin = rotary_tables(start + jnp.arange(rows, dtype=jnp.int32))

    mine, shares = out_weight, []
    for axis, count, index in (("groups", gsz, grp), ("ctx", csz, ctx)):
        piece = mine.shape[0] // count
        if piece % 128 == 0:
            mine = lax.dynamic_slice_in_dim(mine, index * piece, piece, 0)
            shares.append((axis, count))
    steps = list(range(1, zc))
    batches = [steps[1::3], steps[2::3], steps[0::3]]
    moved, far = {}, {}

    def move(batch, *event):
        pieces = [lax.dynamic_slice_in_dim(mine, (z + k) % zc * cols, cols, 1) for k in batch]
        for k, piece in zip(batch, _after(pieces, event)):
            moved[k] = _permute(piece, "tp", [(s, (s + k * yc) % n_tp) for s in range(n_tp)])
            far[k] = [moved[k]], [jnp.int32(0)]

    def share(batch, level, *event):
        if level < len(shares):
            for k in batch:
                arrays, places = far[k]
                far[k] = _spread(_after(arrays, event), places, *shares[level])

    def arrived(batch):
        return [a for k in batch for a in far[k][0]]

    g0, ids = gather_tp(hidden_in[halves[0]], zc, yc)
    a1 = next(g0)
    g1, _ = gather_tp(_after([hidden_in[halves[1]]], [a1])[0], zc, yc)
    a2 = g0.send(a1)
    b1 = next(g1)
    a3 = g0.send(a2)
    b2 = g1.send(b1)
    move(batches[0], a3, b2)
    first = g0.send(a3)
    b3 = g1.send(b2)
    event = [b3] + arrived(batches[0])
    move(batches[1], *event)
    share(batches[0], 0, *event)
    second = g1.send(event)

    def queries_of(c, blocks):
        return project_queries(blocks, ids, attn_gain, query_weight, cos[halves[c]], sin[halves[c]])

    def heard_by(c, q):
        own = attend(q, all_keys, all_values, (start + c * size).reshape(1), span)
        return [own] + [_permute(own, "tp", [(s, (s + k * yc) % n_tp) for s in range(n_tp)]) for k in range(1, zc)]

    q = queries_of(0, first)
    move(batches[2], q)
    heard = [heard_by(0, q)]
    done = heard[0][0]
    share(batches[1], 0, done)
    share(batches[0], 1, done)
    q = queries_of(1, _after(second, [done]))
    share(batches[2], 0, q)
    heard.append(heard_by(1, q))
    done = heard[1][0]
    share(batches[1], 1, done)
    share(batches[2], 1, done)
    heard[0] = _after(heard[0], [done])
    places = far[1][1]
    far = [far[k][0] for k in steps]

    tile = 2 * HB
    h = hadamard_table(HB)
    zero = jnp.zeros_like(h)
    table = jnp.concatenate([jnp.concatenate([h, zero], 1), jnp.concatenate([zero, h], 1)], 0).astype(jnp.bfloat16)
    bits = sign_bits.reshape(1, d)

    def code_half(c, side, out_type):
        return code_terms(heard[c], out_weight, far, places, table, bits, attn_exps, c, z, side, out_type)

    def residual_of(c, sent, mine_sum):
        theirs = _permute(sent, "tp", [(s, s ^ 1) for s in range(n_tp)])
        return add_residual(mine_sum, theirs, hidden_in, table, bits, attn_exps, c, tp)

    residual = residual_of(0, code_half(0, 1 - y, jnp.bfloat16), code_half(0, y, jnp.float32))
    g0, ids = gather_tp(residual, zc, yc)
    a1 = next(g0)
    heard[1] = _after(heard[1], [residual])
    sent = code_half(1, 1 - y, jnp.bfloat16)
    heard[1] = _after(heard[1], [sent, residual])
    residual = residual_of(1, sent, code_half(1, y, jnp.float32))

    g1, _ = gather_tp(_after([residual], [a1])[0], zc, yc)
    a2 = g0.send(a1)
    b1 = next(g1)
    a3 = g0.send(a2)
    b2 = g1.send(b1)
    first = g0.send(a3)
    b3 = g1.send(b2)
    second = g1.send(b3)
    norm_row = norm_gain.reshape(1, d)
    out = norm_rows(first, ids, norm_row, norm_exps, None, 0, rows)
    return norm_rows(second, ids, norm_row, norm_exps, out, 1, rows)


def solution(mesh):
    return jax.shard_map(
        local,
        mesh=mesh,
        in_specs=(
            P(("groups", "ctx"), "tp"),
            P(),
            P(None, "tp"),
            P(("groups", "ctx"), None),
            P(("groups", "ctx"), None),
            P("groups"),
            P("tp", None),
            P(),
            P(("groups", "ctx"), None),
            P(),
            P(("groups", "ctx"), None),
        ),
        out_specs=P(("groups", "ctx"), None),
        check_vma=False,
    )
```

```python
import functools
import math

import jax
import jax.numpy as jnp
from jax import lax
from jax.experimental import pallas as pl
from jax.experimental.pallas import tpu as pltpu
from jax.sharding import PartitionSpec as P

HD = 128
KVH = 4
HB = 128
RB = 32
MIB = 1 << 20
EPS = 1e-05
LOG2E = math.log2(math.e)


def _params(mib, **kw):
    return pltpu.CompilerParams(vmem_limit_bytes=mib * MIB, **kw)


def _cost(flops, moved):
    return pl.CostEstimate(flops=flops // 20, bytes_accessed=moved // 20, transcendentals=0)


def _permute(value, axis, pairs):
    return lax.ppermute(value, axis, pairs)


def _both(value, axis, count):
    if count == 2:
        other = _permute(value, axis, [(0, 1), (1, 0)])
        first = lax.axis_index(axis) == 0
        return jnp.stack([jnp.where(first, value, other), jnp.where(first, other, value)])
    return lax.all_gather(value, axis, axis=0)


def _spread(blocks, places, axis, count):
    if count == 2:
        mate = [_permute(b, axis, [(0, 1), (1, 0)]) for b in blocks]
        return blocks + mate, [2 * p + lax.axis_index(axis) for p in places] + [
            2 * p + 1 - lax.axis_index(axis) for p in places
        ]
    whole = [lax.all_gather(b, axis, axis=0) for b in blocks]
    return [w[i] for w in whole for i in range(count)], [count * p + i for p in places for i in range(count)]


def _after(values, events):
    return list(lax.optimization_barrier((tuple(values), tuple(events)))[0])


class Line:
    def __init__(self, zc, yc):
        self.zc, self.yc, self.n = zc, yc, zc * yc
        self.z = lax.axis_index("tp") // yc
        self.y = lax.axis_index("tp") % yc

    def across(self, v):
        return _permute(v, "tp", [(s, s ^ 1) for s in range(self.n)])

    def up(self, v, k):
        zc, yc = self.zc, self.yc
        return _permute(v, "tp", [(s, s + yc) for s in range(self.n) if k - 1 <= s // yc < zc - 1])

    def down(self, v, k):
        zc, yc = self.zc, self.yc
        return _permute(v, "tp", [(s, s - yc) for s in range(self.n) if 1 <= s // yc <= zc - k])

    def pick(self, a, b, c, d):
        z = self.z
        return jnp.where(z == 0, a, jnp.where(z == 1, b, jnp.where(z == 2, c, d)))

    def ids(self):
        layers = [self.z, self.pick(1, 0, 1, 2), self.pick(2, 2, 3, 1), self.pick(3, 3, 0, 0)]
        y, yc = self.y, self.yc
        return jnp.stack([l * yc + y for l in layers] + [l * yc + (1 - y) for l in layers]).astype(jnp.int32)

    def gather(self, x):
        z, bar = self.z, lax.optimization_barrier
        d1, u1, y0 = bar((self.down(x, 1), self.up(x, 1), self.across(x)))
        va = jnp.where(z == 0, d1, u1)
        (va, u1, d1), _ = bar(((va, u1, d1), (yield y0)))
        d2, u2, ya = bar((self.down(d1, 2), self.up(u1, 2), self.across(va)))
        vb = jnp.where(z == 0, d2, jnp.where(z == 3, u2, d1))
        (vb, u2, d2), _ = bar(((vb, u2, d2), (yield ya)))
        d3, u3, yb = bar((self.down(d2, 3), self.up(u2, 3), self.across(vb)))
        vc = jnp.where(z == 0, d3, jnp.where(z == 1, d2, jnp.where(z == 2, u2, u3)))
        (vc,), _ = bar(((vc,), (yield yb)))
        yield [x, va, vb, vc, y0, ya, yb, self.across(vc)]


def gather_tp(value, zc, yc):
    if zc == 4 and yc == 2:
        line = Line(zc, yc)
        return line.gather(value), line.ids()
    n = zc * yc

    def steps():
        whole = lax.all_gather(value, "tp", axis=0)
        yield whole
        yield whole
        yield whole
        yield [whole[i] for i in range(n)]

    return steps(), jnp.arange(n, dtype=jnp.int32)


def _squares(parts):
    total = None
    for p in parts:
        for c in range(0, p.shape[1], 128):
            f = p[:, c : c + 128].astype(jnp.float32)
            total = f * f if total is None else total + f * f
    return jnp.sum(total, axis=1, keepdims=True)


def _query_kernel(n, heads, ids, *refs):
    parts = refs[:n]
    gain, weight, cos, sin, out = refs[n:]
    width = parts[0].shape[1]
    d = n * width
    r = lax.rsqrt(_squares([p[...] for p in parts]) / d + EPS)
    acc = None
    for i in range(n):
        at = ids[i]
        normed = (parts[i][...].astype(jnp.float32) * r * gain[at]).astype(jnp.bfloat16)
        rows = pl.ds(pl.multiple_of(at * width, width), width)
        t = jnp.dot(normed, weight[rows, :], preferred_element_type=jnp.float32)
        acc = t if acc is None else acc + t
    for h in range(heads):
        v = acc[:, h * HD : (h + 1) * HD]
        turned = v * cos[...] + pltpu.roll(v, HD // 2, 1) * sin[...]
        out[h] = turned.astype(jnp.bfloat16)


def project_queries(blocks, ids, gain, weight, cos, sin):
    n = len(blocks)
    rows, part = blocks[0].shape
    d, width = weight.shape
    heads = width // HD
    tile = min(256, rows)
    gains = gain.astype(jnp.float32).reshape(n, 1, part)
    grid_spec = pltpu.PrefetchScalarGridSpec(
        num_scalar_prefetch=1,
        grid=(rows // tile,),
        in_specs=[pl.BlockSpec((tile, part), lambda i, ids: (i, 0))] * n
        + [
            pl.BlockSpec((n, 1, part), lambda i, ids: (0, 0, 0)),
            pl.BlockSpec((d, width), lambda i, ids: (0, 0), pipeline_mode=pl.Buffered(1)),
            pl.BlockSpec((tile, HD), lambda i, ids: (i, 0)),
            pl.BlockSpec((tile, HD), lambda i, ids: (i, 0)),
        ],
        out_specs=pl.BlockSpec((heads, tile, HD), lambda i, ids: (0, i, 0)),
    )
    return pl.pallas_call(
        functools.partial(_query_kernel, n, heads),
        grid_spec=grid_spec,
        out_shape=jax.ShapeDtypeStruct((heads, rows, HD), jnp.bfloat16),
        compiler_params=_params(48),
        cost_estimate=_cost(2 * rows * d * width, 2 * (rows * d + d * width)),
        name="query_projection",
    )(ids, *blocks, gains, weight, cos, sin)


CK = 1024


def _attend_kernel(heads, tile, span, info, q_ref, k_ref, v_ref, out, s_ref, m_ref, l_ref, acc_ref):
    scale = LOG2E / math.sqrt(HD)
    m = heads * tile
    chunks = span // CK
    tiles = q_ref.shape[1] // tile
    blocks = k_ref.shape[0] // span

    def queries(t):
        return q_ref[:, t * tile : (t + 1) * tile, :].reshape(m, HD)

    def extent(t, b):
        if b == 0:
            return chunks, chunks
        first = info[0] + t * tile - b * span
        return jnp.clip((first + 1) // CK, 0, chunks), jnp.clip((first + tile - 1) // CK + 1, 0, chunks)

    def scores(q, t, b, slot, j, masked):
        keys = k_ref[pl.ds(pl.multiple_of(b * span + j * CK, CK), CK), :]
        s = lax.dot_general(q, keys, (((1,), (1,)), ((), ())), preferred_element_type=jnp.float32)
        if masked:
            row = lax.rem(lax.broadcasted_iota(jnp.int32, (m, CK), 0), tile)
            col = lax.broadcasted_iota(jnp.int32, (m, CK), 1)
            s = jnp.where(col - row <= info[0] + t * tile - b * span - j * CK, s, -1e30)
        s_ref[slot, :, pl.ds(pl.multiple_of(j * CK, CK), CK)] = s
        top = m_ref[...]
        for c in range(CK // 128):
            top = jnp.maximum(top, s[:, c * 128 : (c + 1) * 128])
        m_ref[...] = top

    def weigh(b, slot, j, top):
        s = s_ref[slot, :, pl.ds(pl.multiple_of(j * CK, CK), CK)]
        p = jnp.exp2((s - top) * scale)
        total = l_ref[...]
        for c in range(CK // 128):
            total = total + p[:, c * 128 : (c + 1) * 128]
        l_ref[...] = total
        vals = v_ref[pl.ds(pl.multiple_of(b * span + j * CK, CK), CK), :]
        acc_ref[...] += jnp.dot(p.astype(jnp.bfloat16), vals, preferred_element_type=jnp.float32)

    def loop(low, high, f):
        if not (isinstance(low, int) and isinstance(high, int) and low >= high):
            lax.fori_loop(low, high, lambda j, c: (f(j), c)[1], 0)

    def least(x, y):
        return min(x, y) if isinstance(x, int) and isinstance(y, int) else jnp.minimum(x, y)

    def most(x, y):
        return max(x, y) if isinstance(x, int) and isinstance(y, int) else jnp.maximum(x, y)

    def phase(ahead, behind):
        full = count = seen = 0
        if ahead:
            t, b, slot = ahead
            q = queries(t)
            full, count = extent(t, b)
            m_ref[...] = jnp.full(m_ref.shape, -1e30, jnp.float32)
        if behind:
            t2, b2, slot2, top = behind
            seen = extent(t2, b2)[1]
            l_ref[...] = jnp.zeros(l_ref.shape, jnp.float32)
            acc_ref[...] = jnp.zeros(acc_ref.shape, jnp.float32)

        def both(masked):
            def step(j):
                scores(q, t, b, slot, j, masked)
                weigh(b2, slot2, j, top)

            return step

        x, y = least(full, seen), least(count, seen)
        if ahead and behind:
            loop(0, x, both(False))
            if b > 0:
                loop(x, y, both(True))
        if ahead:
            loop(x, full, lambda j: scores(q, t, b, slot, j, False))
            if b > 0:
                loop(most(y, full), count, lambda j: scores(q, t, b, slot, j, True))
        if behind:
            loop(y, seen, lambda j: weigh(b2, slot2, j, top))
        new_top = jnp.max(m_ref[...], axis=1, keepdims=True) if ahead else None
        return new_top, (jnp.sum(l_ref[...], axis=1, keepdims=True), acc_ref[...]) if behind else None

    jobs = [(t, b) for t in range(tiles) for b in range(blocks)]
    behind = None
    state = None
    for i, job in enumerate(jobs + [None]):
        slot = i % 2
        top, weighed = phase(job + (slot,) if job else None, behind)
        if weighed:
            t2, b2, _, top2 = behind
            total2, acc2 = weighed
            if b2 == 0:
                state = top2, total2, acc2
            else:
                top1, total1, acc1 = state
                new = jnp.maximum(top1, top2)
                f1 = jnp.exp2((top1 - new) * scale)
                f2 = jnp.exp2((top2 - new) * scale)
                state = new, f1 * total1 + f2 * total2, f1 * acc1 + f2 * acc2
            if b2 == blocks - 1:
                res = (state[2] / state[1]).astype(jnp.bfloat16)
                for h in range(heads):
                    out[t2 * tile : (t2 + 1) * tile, h * HD : (h + 1) * HD] = res[h * tile : (h + 1) * tile]
        behind = job + (slot, top) if job else None


def attend(q, keys, values, start, span):
    heads, rows, _ = q.shape
    tile = min(1024 // heads, rows)
    m = heads * tile
    total = keys.shape[0]
    grid_spec = pltpu.PrefetchScalarGridSpec(
        num_scalar_prefetch=1,
        grid=(1,),
        in_specs=[
            pl.BlockSpec((heads, rows, HD), lambda i, info: (0, 0, 0), pipeline_mode=pl.Buffered(1)),
            pl.BlockSpec((total, HD), lambda i, info: (0, 0), pipeline_mode=pl.Buffered(1)),
            pl.BlockSpec((total, HD), lambda i, info: (0, 0), pipeline_mode=pl.Buffered(1)),
        ],
        out_specs=pl.BlockSpec((rows, heads * HD), lambda i, info: (0, 0)),
        scratch_shapes=[
            pltpu.VMEM((2, m, span), jnp.float32),
            pltpu.VMEM((m, 128), jnp.float32),
            pltpu.VMEM((m, 128), jnp.float32),
            pltpu.VMEM((m, HD), jnp.float32),
        ],
    )
    return pl.pallas_call(
        functools.partial(_attend_kernel, heads, tile, span),
        grid_spec=grid_spec,
        out_shape=jax.ShapeDtypeStruct((rows, heads * HD), jnp.bfloat16),
        compiler_params=_params(48),
        cost_estimate=_cost(4 * heads * rows * total * HD, 4 * total * HD),
        name="attend",
    )(start, q, keys, values)


def _spin(x, table):
    hi = x.astype(jnp.bfloat16)
    lo = (x - hi.astype(jnp.float32)).astype(jnp.bfloat16)
    return jnp.dot(hi, table, preferred_element_type=jnp.float32) + jnp.dot(
        lo, table, preferred_element_type=jnp.float32
    )


def _spread_exps(exps, first, width):
    count = exps.shape[1]
    shape = (count, width)
    at = first + lax.broadcasted_iota(jnp.int32, shape, 1) // HB
    pick = jnp.where(lax.broadcasted_iota(jnp.int32, shape, 0) == at, 1.0, 0.0).astype(jnp.bfloat16)
    return jnp.dot(exps.astype(jnp.float32).astype(jnp.bfloat16), pick, preferred_element_type=jnp.float32)


def _signs(bits):
    return (2 * bits - 1).astype(jnp.float32)


def _by_row_block(x, scale):
    blocks = scale.shape[0]
    rows, cols = x.shape
    return (x.reshape(blocks, rows // blocks, cols) * scale[:, None, :]).reshape(rows, cols)


def _code_kernel(zc, pieces, first, blocks, info, *refs):
    atts = refs[:zc]
    own = refs[zc]
    far = refs[zc + 1 : zc + 1 + (zc - 1) * pieces]
    table, bits, exps, out = refs[zc + 1 + (zc - 1) * pieces :]
    tile = table.shape[0]
    sign = _signs(bits[...])
    column = (info[0] + pl.program_id(0)) * (tile // HB)
    scale = jnp.exp2(-_spread_exps(exps[first : first + blocks, :], column, tile)) * (1.0 / math.sqrt(HB))
    piece = far[0].shape[0]
    parts = []
    for k in range(zc):
        if k == 0:
            a, w = atts[0][...], own[...]
        else:
            a = jnp.concatenate(
                [atts[k][:, pl.ds(pl.multiple_of(info[2 + p] * piece, piece), piece)] for p in range(pieces)], axis=1
            )
            w = jnp.concatenate([f[...] for f in far[(k - 1) * pieces : k * pieces]], axis=0)
        parts.append(jnp.dot(a, w, preferred_element_type=jnp.float32) * sign)
    rows = parts[0].shape[0]
    spun = _spin(jnp.concatenate(parts, axis=0), table[...])
    total = None
    for k in range(zc):
        coded = jnp.clip(_by_row_block(spun[k * rows : (k + 1) * rows], scale), -127.0, 127.0)
        coded = coded.astype(jnp.bfloat16).astype(jnp.float32)
        total = coded if total is None else total + coded
    out[...] = total.astype(out.dtype)


def code_terms(atts, own, far, places, table, bits, exps, chunk, z, side, out_type):
    zc = len(atts)
    rows, depth = atts[0].shape
    piece, cols = far[0][0].shape
    pieces = len(far[0])
    width = cols // 2
    tile = table.shape[0]
    steps = width // tile
    blocks = rows // RB
    info = jnp.stack([z * (cols // tile) + side * steps, side * steps] + places).astype(jnp.int32)
    grid_spec = pltpu.PrefetchScalarGridSpec(
        num_scalar_prefetch=1,
        grid=(steps,),
        in_specs=[pl.BlockSpec((rows, depth), lambda j, info: (0, 0), pipeline_mode=pl.Buffered(1))] * zc
        + [pl.BlockSpec((depth, tile), lambda j, info: (0, info[0] + j))]
        + [pl.BlockSpec((piece, tile), lambda j, info: (0, info[1] + j))] * (pieces * len(far))
        + [
            pl.BlockSpec((tile, tile), lambda j, info: (0, 0)),
            pl.BlockSpec((1, tile), lambda j, info: (0, info[0] + j)),
            pl.BlockSpec(exps.shape, lambda j, info: (0, 0)),
        ],
        out_specs=pl.BlockSpec((rows, tile), lambda j, info: (0, j)),
    )
    return pl.pallas_call(
        functools.partial(_code_kernel, zc, pieces, chunk * blocks, blocks),
        grid_spec=grid_spec,
        out_shape=jax.ShapeDtypeStruct((rows, width), out_type),
        compiler_params=_params(48),
        cost_estimate=_cost(2 * zc * rows * width * (depth + 2 * tile), 2 * zc * depth * width),
        name="code_terms",
    )(info, *atts, own, *[f for fs in far for f in fs], table, bits, exps)


def _residual_kernel(first, blocks, info, mine, theirs, hidden, table, bits, exps, out):
    summed = mine[...] + theirs[...].astype(jnp.float32)
    tile = table.shape[0]
    width = summed.shape[1]
    scale = jnp.exp2(_spread_exps(exps[first : first + blocks, :], info[0] * (width // HB), width))
    scale = scale * (1.0 / math.sqrt(HB))
    sign = _signs(bits[...])
    for j in range(width // tile):
        at = slice(j * tile, (j + 1) * tile)
        spun = _spin(summed[:, at], table[...])
        projected = _by_row_block(spun, scale[:, at]) * sign[:, at]
        out[:, at] = (hidden[:, at].astype(jnp.float32) + projected).astype(jnp.bfloat16)


def add_residual(mine, theirs, hidden, table, bits, exps, chunk, tp):
    rows, width = mine.shape
    blocks = rows // RB
    grid_spec = pltpu.PrefetchScalarGridSpec(
        num_scalar_prefetch=1,
        grid=(1,),
        in_specs=[
            pl.BlockSpec((rows, width), lambda i, info: (0, 0)),
            pl.BlockSpec((rows, width), lambda i, info: (0, 0)),
            pl.BlockSpec((rows, width), lambda i, info: (chunk, 0)),
            pl.BlockSpec(table.shape, lambda i, info: (0, 0)),
            pl.BlockSpec((1, width), lambda i, info: (0, info[0])),
            pl.BlockSpec(exps.shape, lambda i, info: (0, 0)),
        ],
        out_specs=pl.BlockSpec((rows, width), lambda i, info: (0, 0)),
    )
    return pl.pallas_call(
        functools.partial(_residual_kernel, chunk * blocks, blocks),
        grid_spec=grid_spec,
        out_shape=jax.ShapeDtypeStruct((rows, width), jnp.bfloat16),
        compiler_params=_params(48),
        cost_estimate=_cost(4 * rows * width * table.shape[0], 10 * rows * width),
        name="residual",
    )(tp.astype(jnp.int32).reshape(1), mine, theirs, hidden, table, bits, exps)


def _norm_kernel(n, ids, *refs):
    parts = refs[:n]
    gain, exps, out = refs[n], refs[n + 1], refs[-1]
    rows, width = parts[0].shape
    d = n * width
    r = lax.rsqrt(_squares([p[...] for p in parts]) / d + EPS)
    blocks = exps.shape[1]
    for i in range(n):
        at = ids[i]
        columns = pl.ds(pl.multiple_of(at * width, width), width)
        e = _spread_exps(exps[0], at * (width // HB), width)
        scaled = parts[i][...].astype(jnp.float32) * r
        g = gain[:, columns].astype(jnp.float32) * jnp.exp2(-e)
        code = jnp.clip(_by_row_block(scaled, g), -127.0, 127.0).astype(jnp.bfloat16)
        value = code.reshape(blocks, rows // blocks, width) * jnp.exp2(e).astype(jnp.bfloat16)[:, None, :]
        out[:, columns] = value.reshape(rows, width)


def norm_rows(blocks, ids, gain, exps, done, chunk, whole):
    n = len(blocks)
    rows, part = blocks[0].shape
    d = n * part
    tile = 128
    steps = rows // tile
    rb = tile // RB
    earlier = [] if done is None else [done]
    grid_spec = pltpu.PrefetchScalarGridSpec(
        num_scalar_prefetch=1,
        grid=(steps,),
        in_specs=[pl.BlockSpec((tile, part), lambda i, ids: (i, 0))] * n
        + [
            pl.BlockSpec((1, d), lambda i, ids: (0, 0)),
            pl.BlockSpec((1, rb, exps.shape[1]), lambda i, ids: (chunk * steps + i, 0, 0)),
        ]
        + [pl.BlockSpec(memory_space=pl.ANY)] * len(earlier),
        out_specs=pl.BlockSpec((tile, d), lambda i, ids: (chunk * steps + i, 0)),
    )
    return pl.pallas_call(
        functools.partial(_norm_kernel, n),
        grid_spec=grid_spec,
        out_shape=jax.ShapeDtypeStruct((whole, d), jnp.bfloat16),
        input_output_aliases={n + 3: 0} if earlier else {},
        compiler_params=_params(60),
        cost_estimate=_cost(8 * rows * d, 4 * rows * d),
        name="norm",
    )(ids, *blocks, gain, exps.reshape(-1, rb, exps.shape[1]), *earlier)


def hadamard_table(order):
    table = jnp.ones((1, 1), dtype=jnp.float32)
    while table.shape[0] < order:
        upper = jnp.concatenate([table, table], axis=1)
        lower = jnp.concatenate([table, -table], axis=1)
        table = jnp.concatenate([upper, lower], axis=0)
    return table


def rotary_tables(positions):
    half = HD // 2
    inv_freq = jnp.exp(-(jnp.arange(half, dtype=jnp.float32) * (2.0 / HD)) * math.log(500000.0))
    angles = positions.astype(jnp.float32)[:, None] * inv_freq[None, :]
    cos, sin = jnp.cos(angles), jnp.sin(angles)
    return jnp.concatenate([cos, cos], axis=1), jnp.concatenate([-sin, sin], axis=1)


def local(
    hidden_in,
    attn_gain,
    query_weight,
    keys,
    values,
    offset,
    out_weight,
    sign_bits,
    attn_exps,
    norm_gain,
    norm_exps,
):
    n_tp, csz, gsz = lax.axis_size("tp"), lax.axis_size("ctx"), lax.axis_size("groups")
    yc = 2 if n_tp % 2 == 0 else 1
    zc = n_tp // yc
    tp, ctx, grp = lax.axis_index("tp"), lax.axis_index("ctx"), lax.axis_index("groups")
    z, y = tp // yc, tp % yc
    rows, width = hidden_in.shape
    d = width * n_tp
    heads = query_weight.shape[1] // HD
    all_heads = heads * n_tp
    depth = out_weight.shape[0]
    cols = d // zc

    column = tp * heads // (all_heads // KVH) * HD
    own_keys = lax.dynamic_slice_in_dim(keys, column, HD, 1)
    own_values = lax.dynamic_slice_in_dim(values, column, HD, 1)
    span = keys.shape[0]
    all_keys = _both(own_keys, "ctx", csz).reshape(csz * span, HD)
    all_values = _both(own_values, "ctx", csz).reshape(csz * span, HD)

    size = rows // 2
    blocks_per = size // RB
    halves = [slice(0, size), slice(size, rows)]
    start = (offset[0] + ctx * rows).astype(jnp.int32)
    cos, sin = rotary_tables(start + jnp.arange(rows, dtype=jnp.int32))

    mine, shares = out_weight, []
    for axis, count, index in (("groups", gsz, grp), ("ctx", csz, ctx)):
        piece = mine.shape[0] // count
        if piece % 128 == 0:
            mine = lax.dynamic_slice_in_dim(mine, index * piece, piece, 0)
            shares.append((axis, count))
    steps = list(range(1, zc))
    batches = [steps[1::3], steps[2::3], steps[0::3]]
    moved, far = {}, {}

    def move(batch, *event):
        pieces = [lax.dynamic_slice_in_dim(mine, (z + k) % zc * cols, cols, 1) for k in batch]
        for k, piece in zip(batch, _after(pieces, event)):
            moved[k] = _permute(piece, "tp", [(s, (s + k * yc) % n_tp) for s in range(n_tp)])
            far[k] = [moved[k]], [jnp.int32(0)]

    def share(batch, level, *event):
        if level < len(shares):
            for k in batch:
                arrays, places = far[k]
                far[k] = _spread(_after(arrays, event), places, *shares[level])

    def arrived(batch):
        return [a for k in batch for a in far[k][0]]

    g0, ids = gather_tp(hidden_in[halves[0]], zc, yc)
    a1 = next(g0)
    g1, _ = gather_tp(_after([hidden_in[halves[1]]], [a1])[0], zc, yc)
    a2 = g0.send(a1)
    b1 = next(g1)
    a3 = g0.send(a2)
    b2 = g1.send(b1)
    move(batches[0], a3, b2)
    first = g0.send(a3)
    b3 = g1.send(b2)
    event = [b3] + arrived(batches[0])
    move(batches[1], *event)
    share(batches[0], 0, *event)
    second = g1.send(event)

    def queries_of(c, blocks):
        return project_queries(blocks, ids, attn_gain, query_weight, cos[halves[c]], sin[halves[c]])

    def heard_by(c, q):
        own = attend(q, all_keys, all_values, (start + c * size).reshape(1), span)
        return [own] + [_permute(own, "tp", [(s, (s + k * yc) % n_tp) for s in range(n_tp)]) for k in range(1, zc)]

    q = queries_of(0, first)
    move(batches[2], q)
    heard = [heard_by(0, q)]
    done = heard[0][0]
    share(batches[1], 0, done)
    share(batches[0], 1, done)
    q = queries_of(1, _after(second, [done]))
    share(batches[2], 0, q)
    heard.append(heard_by(1, q))
    done = heard[1][0]
    share(batches[1], 1, done)
    share(batches[2], 1, done)
    heard[0] = _after(heard[0], [done])
    places = far[1][1]
    far = [far[k][0] for k in steps]

    tile = 2 * HB
    h = hadamard_table(HB)
    zero = jnp.zeros_like(h)
    table = jnp.concatenate([jnp.concatenate([h, zero], 1), jnp.concatenate([zero, h], 1)], 0).astype(jnp.bfloat16)
    bits = sign_bits.reshape(1, d)

    def code_half(c, side, out_type):
        return code_terms(heard[c], out_weight, far, places, table, bits, attn_exps, c, z, side, out_type)

    def residual_of(c, sent, mine_sum):
        theirs = _permute(sent, "tp", [(s, s ^ 1) for s in range(n_tp)])
        return add_residual(mine_sum, theirs, hidden_in, table, bits, attn_exps, c, tp)

    residual = residual_of(0, code_half(0, 1 - y, jnp.bfloat16), code_half(0, y, jnp.float32))
    g0, ids = gather_tp(residual, zc, yc)
    a1 = next(g0)
    heard[1] = _after(heard[1], [residual])
    sent = code_half(1, 1 - y, jnp.bfloat16)
    heard[1] = _after(heard[1], [sent, residual])
    residual = residual_of(1, sent, code_half(1, y, jnp.float32))

    g1, _ = gather_tp(_after([residual], [a1])[0], zc, yc)
    a2 = g0.send(a1)
    b1 = next(g1)
    a3 = g0.send(a2)
    b2 = g1.send(b1)
    first = g0.send(a3)
    b3 = g1.send(b2)
    second = g1.send(b3)
    norm_row = norm_gain.reshape(1, d)
    out = norm_rows(first, ids, norm_row, norm_exps, None, 0, rows)
    return norm_rows(second, ids, norm_row, norm_exps, out, 1, rows)


def solution(mesh):
    return jax.shard_map(
        local,
        mesh=mesh,
        in_specs=(
            P(("groups", "ctx"), "tp"),
            P(),
            P(None, "tp"),
            P(("groups", "ctx"), None),
            P(("groups", "ctx"), None),
            P("groups"),
            P("tp", None),
            P(),
            P(("groups", "ctx"), None),
            P(),
            P(("groups", "ctx"), None),
        ),
        out_specs=P(("groups", "ctx"), None),
        check_vma=False,
    )
```
